128 devices in a mesh: cache: 8 (over z, core), head: 16 (over x, y).
Axes of the slice: x: 4, y: 4, z: 4, core: 2. Of those that a mesh axis runs over, the one named last changes fastest.
Arguments:
- delta_query: bfloat16 [32, 512, 2048], P('cache', None, 'head'), may hold values from -6 to 6
- delta_key: bfloat16 [32, 512, 2048], P('cache', None, 'head'), may hold values from -6 to 6
- delta_value: bfloat16 [32, 512, 4096], P('cache', None, 'head'), may hold values from -6 to 6
- delta_gate: bfloat16 [32, 512, 4096], P('cache', None, 'head'), may hold values from -6 to 6
- write_strength: float32 [32, 32, 512], P('cache', 'head'), may hold values from 0.1 to 0.95
- decay_log: float32 [32, 32, 512], P('cache', 'head'), may hold values from -1.5 to 0
- kept_state: float32 [32, 32, 128, 128], P('cache', 'head'), may hold values from -6 to 6
- kept_kv: bfloat16 [32, 1024, 2, 512], P('cache', 'head'), may hold values from -8 to 8
- fresh_kv: bfloat16 [32, 512, 2, 512], P('cache', 'head'), may hold values from -6 to 6
- attn_query: bfloat16 [32, 512, 4096], P('cache', None, 'head'), may hold values from -100 to 100
- attn_gate: bfloat16 [32, 512, 4096], P('cache', None, 'head'), may hold values from -6 to 6
- cached_len: int32 [32], replicated, may hold values from 2 to 1024, as said below
- slot_of_session: int32 [32], replicated, may hold values from 0 to 31, as said below
- delta_out_weight: bfloat16 [4096, 2048], P('head'), may hold values from -0.09375 to 0.09375
- attn_out_weight: bfloat16 [4096, 2048], P('head'), may hold values from -0.75 to 0.75
Outputs:
- delta_mixed: bfloat16 [16384, 2048], P(('cache', 'head'))
- attn_mixed: bfloat16 [16384, 2048], P(('cache', 'head'))
- final_state: float32 [32, 32, 128, 128], P('cache', 'head')
The draws below stay inside these ranges and needn't reach their ends.
Inputs may be any that keep to these rules, and one draw needn't show every extreme that they name: `slot_of_session`: a permutation of the slots; slot r lies on cache shard floor(r / 4); session s belongs to owner floor(s / 4), and the 4 sessions of one owner are kept on 4 different shards. `cached_len`: some session keeps exactly 1024 positions.
All inputs are finite; a program needn't handle non-finite values.
Results may differ from the reference program's by a relative error of at most 0.02.
Values may be sent and summed in bfloat16 or wider, within the bound.
No kernel may reach another device: no remote copies, remote signals or barrier semaphores. Data moves between devices by JAX's collectives and lax.ppermute only.
A program may use at most 128 MiB of HBM per device.

```python
import math
import jax
import jax.numpy as jnp
from jax import lax

D = 2048
LQH = 16
LVH = 32
LK = 128
LV = 128
AH = 16
KVH = 2
HD = 256
NEW = 512
SESS_DEV = 4
LMAX = 1024
SESSIONS = 32
N_CACHE = 8
N_HEAD = 16


def draw_kept_kv(key, part):
    key = jax.random.fold_in(key, 7)
    cache = jax.random.truncated_normal(key, -6.0, 6.0, (SESSIONS, LMAX, 2, KVH * HD), jnp.float32)
    return cache.astype(jnp.bfloat16)


def draw_attn_query(key, part):
    key = jax.random.fold_in(key, 9)
    query_matrix = 1.5 * jax.random.truncated_normal(key, -6.0, 6.0, (SESSIONS, NEW, AH, HD), jnp.float32)
    return query_matrix.reshape(SESSIONS, NEW, AH * HD).astype(jnp.bfloat16)


def draw_cached_len(key, part):
    key = jax.random.fold_in(key, 3)
    first_key, second_key = jax.random.split(key)
    lengths = jax.random.randint(first_key, (SESSIONS,), 2, LMAX + 1)
    longest = jax.random.randint(second_key, (), 0, SESSIONS)
    return jnp.where(jnp.arange(SESSIONS) == longest, LMAX, lengths).astype(jnp.int32)


def draw_slot_of_session(key, part):
    key = jax.random.fold_in(key, 5)
    keys = jax.random.split(key, 4)
    owner_perm = jax.random.permutation(keys[0], N_CACHE)
    shard_perm = jax.random.permutation(keys[1], N_CACHE)
    shifts = jax.random.permutation(keys[2], N_CACHE)[:SESS_DEV]
    session_ids = jnp.arange(SESSIONS)
    owners = session_ids // SESS_DEV
    local = session_ids % SESS_DEV
    shard = shard_perm[(owner_perm[owners] + shifts[local]) % N_CACHE]
    within = jax.vmap(lambda sub: jax.random.permutation(sub, SESS_DEV))(jax.random.split(keys[3], N_CACHE))
    return (shard * SESS_DEV + within[shard, local]).astype(jnp.int32)


def draw_decay_log(key, part):
    key = jax.random.fold_in(key, 11)
    keys = jax.random.split(key, 5)
    shape_two = (SESSIONS, LVH)
    fast_cut = 5
    fast = jax.random.randint(keys[0], shape_two, 0, 10) < fast_cut
    fast_rate = jnp.exp(jax.random.uniform(keys[1], shape_two, jnp.float32, jnp.log(1.0 / 50.0), jnp.log(1.0 / 30.0)))
    slow_rate = jnp.exp(jax.random.uniform(keys[2], shape_two, jnp.float32, jnp.log(0.05 / NEW), jnp.log(0.5 / NEW)))
    forgetting_factor = jnp.where(fast, fast_rate, slow_rate)
    stored_entry_places = jax.random.randint(keys[3], shape_two + (2,), 0, NEW)
    objective_scores = jnp.log(jax.random.uniform(keys[4], shape_two + (2,), jnp.float32, 0.5, 0.8))
    sequence_offset = jnp.arange(NEW)
    prompt_segments = jnp.sum(jnp.where(sequence_offset[None, None, None, :] == stored_entry_places[..., None], objective_scores[..., None], 0.0), axis=2)
    return (prompt_segments - forgetting_factor[..., None]).astype(jnp.float32)


def levels(rng, extent, cuts, low, top_value):
    level, own = 1.0, jax.random.fold_in(rng, 6)
    for axis_at, blocks in cuts:
        draws = jnp.exp(jax.random.uniform(jax.random.fold_in(own, axis_at), (blocks,), jnp.float32, low / len(cuts), top_value / len(cuts)))
        level = level * jnp.repeat(draws, extent[axis_at] // blocks).reshape([-1 if axis == axis_at else 1 for axis in range(len(extent))])
    return level


def noise(stream_key, dims, deviation, reach, cuts=(), kind=jnp.bfloat16):
    drawn = deviation * jax.random.normal(stream_key, dims, jnp.float32)
    if cuts:
        drawn = drawn * levels(stream_key, dims, cuts, -0.22, 0.18)
    return jnp.clip(drawn, -reach, reach).astype(kind)


def setup_inputs(seed: int = 0) -> dict:
    streams_of = jax.random.split(jax.random.key(seed), 16)
    return {
        "delta_query": noise(streams_of[0], (SESSIONS, NEW, LQH * LK), 1.0, 6.0, ((0, 8), (2, 16))),
        "delta_key": noise(streams_of[1], (SESSIONS, NEW, LQH * LK), 1.0, 6.0, ((0, 8), (2, 16))),
        "delta_value": noise(streams_of[2], (SESSIONS, NEW, LVH * LV), 1.0, 6.0, ((0, 8), (2, 16))),
        "delta_gate": noise(streams_of[3], (SESSIONS, NEW, LVH * LV), 1.0, 6.0, ((0, 8), (2, 16))),
        "write_strength": jnp.clip(0.1 + 0.84999999 * jax.random.uniform(streams_of[4], (SESSIONS, LVH, NEW), jnp.float32) ** levels(streams_of[4], (SESSIONS, LVH, NEW), ((0, 8), (1, 16)), -0.2, 0.2), 0.1, 0.95),
        "decay_log": draw_decay_log(jax.random.fold_in(streams_of[15], 71), 0),
        "kept_state": noise(streams_of[6], (SESSIONS, LVH, LK, LV), 1.0, 6.0, ((0, 8), (1, 16)), jnp.float32),
        "kept_kv": draw_kept_kv(jax.random.fold_in(streams_of[15], 71), 0),
        "fresh_kv": noise(streams_of[8], (SESSIONS, NEW, 2, KVH * HD), 1.0, 6.0, ((0, 8), (1, 16))),
        "attn_query": draw_attn_query(jax.random.fold_in(streams_of[15], 71), 0),
        "attn_gate": noise(streams_of[10], (SESSIONS, NEW, AH * HD), 1.0, 6.0, ((0, 8), (2, 16))),
        "cached_len": draw_cached_len(jax.random.fold_in(streams_of[15], 71), 0),
        "slot_of_session": draw_slot_of_session(jax.random.fold_in(streams_of[15], 71), 0),
        "delta_out_weight": noise(streams_of[13], (LVH * LV, D), (LVH * LV) ** -0.5, 0.09375, ((0, 16),)),
        "attn_out_weight": noise(streams_of[14], (AH * HD, D), (HD // 4) ** -0.5, 0.75, ((0, 16),)),
    }


def unit_rows(matrix, epsilon):
    return matrix / jnp.sqrt(lax.optimization_barrier(jnp.sum(matrix * matrix, axis=-1, keepdims=True)) + epsilon)

def project_heads(heads, weight):
    group_cols = heads.shape[1] // N_HEAD
    aggregate_total = jnp.zeros((heads.shape[0], weight.shape[1]), jnp.float32)
    for group_id in range(N_HEAD):
        product_part = jnp.dot(heads[:, group_id * group_cols:(group_id + 1) * group_cols], weight[group_id * group_cols:(group_id + 1) * group_cols], preferred_element_type=jnp.float32)
        rounded = lax.optimization_barrier(product_part.astype(jnp.bfloat16))
        aggregate_total = aggregate_total + rounded.astype(jnp.float32)
    return aggregate_total.astype(jnp.bfloat16)

def delta_layer(delta_query, delta_key, delta_value, delta_gate, write_strength, decay_log, state_start):
    count = delta_query.shape[0]
    share_ratio = LVH // LQH
    query_matrix = unit_rows(delta_query.astype(jnp.float32).reshape(count, NEW, LQH, LK), 1e-06) * (1.0 / math.sqrt(LK))
    keyed = unit_rows(delta_key.astype(jnp.float32).reshape(count, NEW, LQH, LK), 1e-06)
    query_matrix = jnp.repeat(query_matrix, share_ratio, axis=2).transpose(1, 0, 2, 3)
    keyed = jnp.repeat(keyed, share_ratio, axis=2).transpose(1, 0, 2, 3)
    values = delta_value.astype(jnp.float32).reshape(count, NEW, LVH, LV).transpose(1, 0, 2, 3)
    strengths = write_strength.transpose(2, 0, 1)
    decays = decay_log.transpose(2, 0, 1)

    def advance(carried, pieces):
        q_now, k_now, v_now, b_now, g_now = pieces
        carried = jnp.exp(g_now)[:, :, None, None] * carried
        guess = jnp.einsum('shkv,shk->shv', carried, k_now, precision=lax.Precision.HIGHEST)
        update = b_now[:, :, None] * (v_now - guess)
        carried = carried + k_now[:, :, :, None] * update[:, :, None, :]
        emitted = jnp.einsum('shkv,shk->shv', carried, q_now, precision=lax.Precision.HIGHEST)
        return (carried, emitted)
    final_state, emitted = lax.scan(advance, state_start, (query_matrix, keyed, values, strengths, decays))
    emitted = emitted.transpose(1, 0, 2, 3)
    normed = emitted / jnp.sqrt(lax.optimization_barrier(jnp.mean(emitted * emitted, axis=-1, keepdims=True)) + 1e-06)
    gate_f = delta_gate.astype(jnp.float32).reshape(count, NEW, LVH, LV)
    heads = (normed * jax.nn.silu(gate_f)).astype(jnp.bfloat16).reshape(count * NEW, LVH * LV)
    return (heads, final_state)

def attend_session(pieces):
    query_rows, gate_rows, cache, fresh, length = pieces
    key_row_matrix = jnp.concatenate([cache[:, 0], fresh[:, 0]], axis=0).astype(jnp.float32).reshape(-1, KVH, HD)
    value_rows = jnp.concatenate([cache[:, 1], fresh[:, 1]], axis=0).astype(jnp.float32).reshape(-1, KVH, HD)
    head_kv = jnp.arange(AH) // (AH // KVH)
    key_row_matrix = key_row_matrix[:, head_kv]
    value_rows = value_rows[:, head_kv]
    query_matrix = query_rows.astype(jnp.float32).reshape(NEW, AH, HD)
    scores = jnp.einsum('thd,lhd->htl', query_matrix, key_row_matrix) * (1.0 / math.sqrt(HD))
    sequence_offset = jnp.arange(LMAX + NEW, dtype=jnp.int32)
    steps_new = jnp.arange(NEW, dtype=jnp.int32)
    usable = jnp.where(sequence_offset[None, :] < LMAX, sequence_offset[None, :] < length, sequence_offset[None, :] - LMAX <= steps_new[:, None])
    masked = jnp.where(usable[None], scores, -1e+30)
    peak_row = lax.optimization_barrier(jnp.max(masked, axis=-1, keepdims=True))
    weights = jnp.where(usable[None], jnp.exp(masked - peak_row), 0.0)
    total_w = lax.optimization_barrier(jnp.sum(weights, axis=-1))
    rounded = lax.optimization_barrier(weights.astype(jnp.bfloat16)).astype(jnp.float32)
    mixed = jnp.einsum('htl,lhd->thd', rounded, value_rows) / total_w.T[:, :, None]
    gated = jax.nn.sigmoid(gate_rows.astype(jnp.float32).reshape(NEW, AH, HD)) * mixed
    return gated.reshape(NEW, AH * HD).astype(jnp.bfloat16)

def reference(delta_query, delta_key, delta_value, delta_gate, write_strength, decay_log, kept_state, kept_kv, fresh_kv, attn_query, attn_gate, cached_len, slot_of_session, delta_out_weight, attn_out_weight):
    slots = slot_of_session.astype(jnp.int32)
    state_start = jnp.take(kept_state, slots, axis=0)
    cache_start = jnp.take(kept_kv, slots, axis=0)
    delta_heads, final_state = delta_layer(delta_query, delta_key, delta_value, delta_gate, write_strength, decay_log, state_start)
    delta_mixed = project_heads(delta_heads, delta_out_weight)
    attn_heads = lax.map(attend_session, (attn_query, attn_gate, cache_start, fresh_kv, cached_len))
    attn_heads = attn_heads.reshape(-1, AH * HD)
    attn_mixed = project_heads(attn_heads, attn_out_weight)
    return (delta_mixed, attn_mixed, final_state)
```

```python
import functools
import math

import jax
import jax.numpy as jnp
import numpy as np
from jax import lax
from jax.experimental import pallas as pl
from jax.experimental.pallas import tpu as pltpu
from jax.sharding import Mesh, PartitionSpec as P

F32 = jnp.float32
BF16 = jnp.bfloat16
CH = 128
HIGH = lax.Precision.HIGHEST
NEG = -1e30
VMEM = 60 * 1024 * 1024


def cost(us):
    return pl.CostEstimate(flops=int(us * 1e9), transcendentals=0, bytes_accessed=int(us * 3e6))


def after(value, *others):
    return lax.optimization_barrier((value, others))[0]


def mm(a, b):
    return lax.dot_general(a, b, (((1,), (0,)), ((), ())), preferred_element_type=F32)


def mm_nt(a, b, precision=None):
    return lax.dot_general(
        a, b, (((1,), (1,)), ((), ())), preferred_element_type=F32, precision=precision
    )


def prep_kernel(q_ref, k_ref, v_ref, b_ref, g_ref, wq_ref, u_ref, p_ref, kt_ref, dec_ref):
    row = lax.broadcasted_iota(jnp.int32, (CH, CH), 0)
    col = lax.broadcasted_iota(jnp.int32, (CH, CH), 1)
    strict = row > col
    incl = row >= col
    diag = row == col
    tri = jnp.where(incl, 1.0, 0.0).astype(F32)
    eye = jnp.where(diag, 1.0, 0.0).astype(F32)
    g8 = jnp.concatenate([g_ref[s] for s in range(4)], axis=0)
    b8 = jnp.concatenate([b_ref[s] for s in range(4)], axis=0)
    g_rows = mm_nt(g8, tri, HIGH)
    g_cols = mm_nt(tri, g8, HIGH)
    b_cols = mm_nt(eye, b8, HIGH)
    chains = []
    for s in range(4):
        k = k_ref[s]
        q = q_ref[s]
        kk = mm_nt(k, k)
        qk = mm_nt(q, k)
        kf = k.astype(F32)
        qf = q.astype(F32)
        rk = lax.rsqrt(jnp.sum(kf * kf, axis=1, keepdims=True) + 1e-6)
        rq = lax.rsqrt(jnp.sum(qf * qf, axis=1, keepdims=True) + 1e-6) * (1.0 / math.sqrt(128.0))
        rk_row = lax.rsqrt(jnp.sum(jnp.where(diag, kk, 0.0), axis=0, keepdims=True) + 1e-6)
        kkn = kk * rk * rk_row
        qkn = qk * rq * rk_row
        kn = kf * rk
        qn = qf * rq
        for h in range(2):
            i = 2 * s + h
            gc = g_cols[:, i : i + 1]
            gr = g_rows[i : i + 1, :]
            bc = b_cols[:, i : i + 1]
            decay = jnp.where(incl, jnp.exp(jnp.where(incl, gc - gr, 0.0)), 0.0)
            low = jnp.where(strict, decay * kkn * bc, 0.0)
            p_ref[0, i] = (decay * qkn).astype(BF16)
            growth = jnp.exp(gc)
            g_last = gr[:, CH - 1 : CH]
            tail = jnp.exp(g_last - gc)
            kt_ref[0, i] = (tail * kn).T.astype(BF16)
            wq_ref[0, i, CH:, :] = (growth * qn).astype(BF16)
            dec_ref[0, i : i + 1, :] = jnp.broadcast_to(jnp.exp(g_last), (1, CH))
            rhs = jnp.concatenate(
                [bc * v_ref[s, :, h * CH : (h + 1) * CH].astype(F32), (bc * growth) * kn], axis=1
            ).astype(BF16)
            chains.append([low, rhs])
    inverses = []
    pair = (row // 2 == col // 2) & strict
    for low, _ in chains:
        inverses.append(eye - jnp.where(pair, low, 0.0))
    m = 2
    while m < CH:
        mask = (row // (2 * m) == col // (2 * m)) & (row // m > col // m)
        lefts = [
            mm(jnp.where(mask, chains[i][0], 0.0).astype(BF16), inverses[i].astype(BF16))
            for i in range(8)
        ]
        steps = [mm(inverses[i].astype(BF16), lefts[i].astype(BF16)) for i in range(8)]
        inverses = [inverses[i] - steps[i] for i in range(8)]
        m *= 2
    for i in range(8):
        solved = mm(inverses[i].astype(BF16), chains[i][1])
        u_ref[0, i] = solved[:, :CH]
        wq_ref[0, i, :CH, :] = solved[:, CH:].astype(BF16)


def prep(delta_query, delta_key, delta_value, strengths, decays):
    chunks = delta_query.shape[1] // CH
    spec_tok = lambda w: pl.BlockSpec((4, CH, w), lambda c: (0, c, 0))
    spec_rate = pl.BlockSpec((4, 2, CH), lambda c: (0, 0, c))
    spec_out = lambda r: pl.BlockSpec((1, 8, r, CH), lambda c: (c, 0, 0, 0))
    shape = lambda r, t: jax.ShapeDtypeStruct((chunks, 8, r, CH), t)
    return pl.pallas_call(
        prep_kernel,
        grid=(chunks,),
        in_specs=[spec_tok(CH), spec_tok(CH), spec_tok(2 * CH), spec_rate, spec_rate],
        out_specs=[
            spec_out(2 * CH),
            spec_out(CH),
            spec_out(CH),
            spec_out(CH),
            pl.BlockSpec((1, 8, CH), lambda c: (c, 0, 0)),
        ],
        out_shape=[
            shape(2 * CH, BF16),
            shape(CH, F32),
            shape(CH, BF16),
            shape(CH, BF16),
            jax.ShapeDtypeStruct((chunks, 8, CH), F32),
        ],
        compiler_params=pltpu.CompilerParams(vmem_limit_bytes=VMEM),
        cost_estimate=cost(0.1),
        name="delta_prep",
    )(delta_query, delta_key, delta_value, strengths, decays)


def scan_kernel(
    src_ref, state_ref, wq_ref, u_ref, p_ref, kt_ref, dec_ref, gate_ref, heads_ref, final_ref, carry
):
    c = pl.program_id(0)

    @pl.when(c == 0)
    def _():
        for s in range(4):
            for h in range(2):
                for j in range(4):
                    block = state_ref[src_ref[s], 32 * h : 32 * h + 32, j * CH : (j + 1) * CH]
                    carry[2 * s + h, 32 * j : 32 * j + 32, :] = block.astype(F32)

    states = [carry[i] for i in range(8)]
    reads = [mm(wq_ref[0, i], states[i].astype(BF16)) for i in range(8)]
    updates = [(u_ref[0, i] - reads[i][:CH]).astype(BF16) for i in range(8)]
    for i in range(8):
        carry[i] = states[i] * dec_ref[0, i : i + 1, :] + mm(kt_ref[0, i], updates[i])
    for i in range(8):
        s, h = i // 2, i % 2
        out = reads[i][CH:] + mm(p_ref[0, i], updates[i])
        scale = lax.rsqrt(jnp.mean(out * out, axis=1, keepdims=True) + 1e-6)
        gate = gate_ref[s, :, h * CH : (h + 1) * CH].astype(F32)
        silu = gate / (1.0 + jnp.exp(-gate))
        heads_ref[0, s, :, h * CH : (h + 1) * CH] = (out * scale * silu).astype(BF16)

    @pl.when(c == pl.num_programs(0) - 1)
    def _():
        for s in range(4):
            for h in range(2):
                final_ref[s, h] = carry[2 * s + h]


def scan(source, arrived, prepared, delta_gate):
    wq, u0, p, kt, dec = prepared
    chunks = wq.shape[0]
    spec = lambda r: pl.BlockSpec((1, 8, r, CH), lambda c, *_: (c, 0, 0, 0))
    return pl.pallas_call(
        scan_kernel,
        grid_spec=pltpu.PrefetchScalarGridSpec(
            num_scalar_prefetch=1,
            grid=(chunks,),
            in_specs=[
                pl.BlockSpec((8, 64, 512), lambda c, *_: (0, 2, 0)),
                spec(2 * CH),
                spec(CH),
                spec(CH),
                spec(CH),
                pl.BlockSpec((1, 8, CH), lambda c, *_: (c, 0, 0)),
                pl.BlockSpec((4, CH, 2 * CH), lambda c, *_: (0, c, 0)),
            ],
            out_specs=[
                pl.BlockSpec((1, 4, CH, 2 * CH), lambda c, *_: (c, 0, 0, 0)),
                pl.BlockSpec((4, 2, CH, CH), lambda c, *_: (0, 0, 0, 0)),
            ],
            scratch_shapes=[pltpu.VMEM((8, CH, CH), F32)],
        ),
        out_shape=[
            jax.ShapeDtypeStruct((chunks, 4, CH, 2 * CH), BF16),
            jax.ShapeDtypeStruct((4, 2, CH, CH), F32),
        ],
        compiler_params=pltpu.CompilerParams(vmem_limit_bytes=VMEM),
        cost_estimate=cost(0.1),
        name="delta_scan",
    )(source, arrived, wq, u0, p, kt, dec, delta_gate)


def swap_halves(core, head):
    low, high = head[:, :CH], head[:, CH:]
    return jnp.concatenate(
        [jnp.where(core == 0, low, high), jnp.where(core == 0, high, low)], axis=1
    )


def delta_project_kernel(sc_ref, heads_ref, own_ref, other_ref, *outs):
    x, y, core = sc_ref[0], sc_ref[1], sc_ref[2]
    total = None
    for e in range(4):
        rows = jnp.concatenate([heads_ref[(y - e) & 3, (x + d) & 3] for d in range(4)], axis=0)
        weight = jnp.concatenate([own_ref[e], other_ref[e]], axis=0)
        part = mm(swap_halves(core, rows), weight)
        total = part if total is None else total + part
    total = total.astype(BF16)
    for d, ref in enumerate(outs):
        ref[...] = total[d * CH : (d + 1) * CH]


def delta_project(scalars, pieces, own, other):
    weight = pl.BlockSpec((4, CH, 512), lambda i, sc: (0, i, 0))
    return pl.pallas_call(
        delta_project_kernel,
        grid_spec=pltpu.PrefetchScalarGridSpec(
            num_scalar_prefetch=1,
            grid=(4,),
            in_specs=[pl.BlockSpec(pieces.shape, lambda i, sc: (0, 0, 0, 0)), weight, weight],
            out_specs=[pl.BlockSpec((CH, 512), lambda i, sc: (0, i))] * 4,
        ),
        out_shape=[jax.ShapeDtypeStruct((CH, 2048), BF16)] * 4,
        compiler_params=pltpu.CompilerParams(vmem_limit_bytes=VMEM),
        cost_estimate=cost(0.1),
        name="delta_project",
    )(scalars, pieces, own, other)


def pack_kernel(sc_ref, q_ref, g_ref, aw_ref, dw_ref, o0, o1, o2, o3, share_ref):
    for k, out in enumerate((o0, o1, o2, o3)):
        j = (sc_ref[0] + k) & 3
        out[:512, :256] = q_ref[j]
        out[:512, 256:] = g_ref[j]
        for n in range(4):
            out[512 + n * CH : 512 + (n + 1) * CH] = aw_ref[:, n * 512 : (n + 1) * 512]
    for n in range(4):
        share_ref[n * CH : (n + 1) * CH] = dw_ref[:, n * 512 : (n + 1) * 512]


def pack(scalars, query, gate, attn_weight, delta_weight):
    whole = pl.BlockSpec(query.shape, lambda i, sc: (0, 0, 0))
    half = pl.BlockSpec((CH, 2048), lambda i, sc: (sc[1], 0))
    return pl.pallas_call(
        pack_kernel,
        grid_spec=pltpu.PrefetchScalarGridSpec(
            num_scalar_prefetch=1,
            grid=(1,),
            in_specs=[whole, whole, half, half],
            out_specs=[pl.BlockSpec((1024, 512), lambda i, sc: (0, 0))] * 4
            + [pl.BlockSpec((512, 512), lambda i, sc: (0, 0))],
        ),
        out_shape=[jax.ShapeDtypeStruct((1024, 512), BF16)] * 4
        + [jax.ShapeDtypeStruct((512, 512), BF16)],
        compiler_params=pltpu.CompilerParams(vmem_limit_bytes=VMEM),
        cost_estimate=cost(0.1),
        name="pack_queries",
    )(scalars, query, gate, attn_weight, delta_weight)


def stack_kernel(r0, r1, r2, r3, out):
    for k, ref in enumerate((r0, r1, r2, r3)):
        out[k] = ref[...]


def stack_rows(arrays, block):
    return pl.pallas_call(
        stack_kernel,
        grid=(1,),
        in_specs=[pl.BlockSpec((512, 512), lambda i: (block, 0))] * 4,
        out_specs=pl.BlockSpec((4, 512, 512), lambda i: (0, 0, 0)),
        out_shape=jax.ShapeDtypeStruct((4, 512, 512), BF16),
        compiler_params=pltpu.CompilerParams(vmem_limit_bytes=VMEM),
        cost_estimate=cost(0.1),
        name="stack_weights",
    )(*arrays)


def select_kernel(src_ref, landed_ref, fresh_ref, out_ref):
    for j in range(4):
        out_ref[j, :CH] = landed_ref[src_ref[j], :CH]
        out_ref[j, CH:] = fresh_ref[j]


def select(source, landed, fresh):
    vmem = pl.BlockSpec(memory_space=pltpu.VMEM)
    return pl.pallas_call(
        select_kernel,
        in_specs=[pl.BlockSpec(memory_space=pltpu.SMEM), vmem, vmem],
        out_specs=vmem,
        out_shape=jax.ShapeDtypeStruct((4, CH + 64, 512), BF16),
        compiler_params=pltpu.CompilerParams(vmem_limit_bytes=VMEM),
        cost_estimate=cost(0.1),
        name="select_sessions",
    )(source, landed, fresh)


def attention_kernel(
    sc_ref, q0, q1, q2, q3, p0, p1, p2, p3, own_hbm, other_hbm, o0, o1, w_ref, w_sem, keys, values, heads
):
    fetches = [
        pltpu.make_async_copy(hbm, w_ref.at[n], w_sem.at[n])
        for n, hbm in enumerate((own_hbm, other_hbm))
    ]
    for fetch in fetches:
        fetch.start()
    y, length = sc_ref[1], sc_ref[2]
    rows = 2 * CH
    at_kept = lax.broadcasted_iota(jnp.int32, (1, 256), 1)
    at_fresh = lax.broadcasted_iota(jnp.int32, (1, 128), 1)
    kept_bias, fresh_place = [], []
    for e, ref in enumerate((p0, p1, p2, p3)):
        from_y = (y - e) & 3
        place = ((at_kept >> 6) * 4 + from_y) * 64 + (at_kept & 63)
        kept_bias.append(jnp.where(place < length, 0.0, NEG))
        fresh_place.append(((at_fresh >> 5) * 4 + from_y) * 32 + (at_fresh & 31))
        for j in range(4):
            kept_at, fresh_at = e * 256 + j * 64, 1024 + e * 128 + j * 32
            keys[kept_at : kept_at + 64] = ref[j, :64]
            values[kept_at : kept_at + 64] = ref[j, 64:128]
            keys[fresh_at : fresh_at + 32] = ref[j, 128:160]
            values[fresh_at : fresh_at + 32] = ref[j, 160:]
    kept_bias = jnp.concatenate(kept_bias, axis=1)
    fresh_place = jnp.concatenate(fresh_place, axis=1)
    token = lax.broadcasted_iota(jnp.int32, (rows, 512), 0) & (CH - 1)
    scale = math.log2(math.e) / 16.0

    def load(n, pair, cols):
        at = pl.ds(pl.multiple_of(sc_ref[3 + n] * CH, CH), CH)
        return jnp.concatenate([r[at, cols] for r in pair], axis=0)

    def score(n, pair):
        query = load(n, pair, slice(0, 256))
        return mm_nt(query, keys[:1024]), mm_nt(query, keys[1024:])

    groups = [(n, g) for n in range(2) for g in range(2)]
    pairs = ((q0, q1), (q2, q3))
    ahead = score(0, pairs[0])
    for step, (n, g) in enumerate(groups):
        kept, fresh = ahead
        if step + 1 < len(groups):
            ahead = score(groups[step + 1][0], pairs[groups[step + 1][1]])
        kept = kept + kept_bias
        fresh = jnp.where(fresh_place <= token + sc_ref[3 + n] * CH, fresh, NEG)
        peak = jnp.maximum(
            jnp.max(kept, axis=1, keepdims=True), jnp.max(fresh, axis=1, keepdims=True)
        )
        kept = jnp.exp2((kept - peak) * scale)
        fresh = jnp.exp2((fresh - peak) * scale)
        total = jnp.sum(kept, axis=1, keepdims=True) + jnp.sum(fresh, axis=1, keepdims=True)
        mixed = mm(kept.astype(BF16), values[:1024]) + mm(fresh.astype(BF16), values[1024:])
        gate = load(n, pairs[g], slice(256, 512)).astype(F32)
        gated = (mixed / (total * (1.0 + jnp.exp(-gate)))).astype(BF16)
        for i in range(2):
            k = 2 * g + i
            heads[n * CH : (n + 1) * CH, k * 256 : (k + 1) * 256] = gated[i * CH : (i + 1) * CH]
    for fetch in fetches:
        fetch.wait()
    gated = [swap_halves(sc_ref[5], heads[:, k * 256 : (k + 1) * 256]) for k in range(4)]
    for j in range(4):
        rows = slice(j * CH, (j + 1) * CH)
        out = sum(
            mm(gated[k], jnp.concatenate([w_ref[0, k, rows], w_ref[1, k, rows]], axis=0))
            for k in range(4)
        ).astype(BF16)
        o0[:, j * 512 : (j + 1) * 512] = out[:CH]
        o1[:, j * 512 : (j + 1) * 512] = out[CH:]


def attention(scalars, queries, positions, own, other):
    whole = lambda a: pl.BlockSpec(a.shape, lambda i, sc: (0,) * a.ndim)
    return pl.pallas_call(
        attention_kernel,
        grid_spec=pltpu.PrefetchScalarGridSpec(
            num_scalar_prefetch=1,
            grid=(1,),
            in_specs=[pl.BlockSpec((512, 512), lambda i, sc: (0, 0))] * 4
            + [whole(a) for a in positions]
            + [pl.BlockSpec(memory_space=pl.ANY)] * 2,
            out_specs=[pl.BlockSpec((CH, 2048), lambda i, sc: (0, 0))] * 2,
            scratch_shapes=[
                pltpu.VMEM((2, 4, 512, 512), BF16),
                pltpu.SemaphoreType.DMA((2,)),
                pltpu.VMEM((1536, 256), BF16),
                pltpu.VMEM((1536, 256), BF16),
                pltpu.VMEM((2 * CH, 1024), BF16),
            ],
        ),
        out_shape=[jax.ShapeDtypeStruct((CH, 2048), BF16)] * 2,
        compiler_params=pltpu.CompilerParams(vmem_limit_bytes=VMEM),
        cost_estimate=cost(0.1),
        name="attention_project",
    )(scalars, *queries, *positions, own, other)


ORDER = (2, 1, 3)


def shift(array, axis, by):
    return lax.ppermute(array, axis, [(i, (i + by) % 4) for i in range(4)])


def row_of(array, index):
    return lax.dynamic_index_in_dim(array, index, 0, keepdims=False)


def all_to_all(array, axis):
    return lax.all_to_all(array, axis, split_axis=0, concat_axis=0, tiled=True)


def sum_over(parts, axis):
    total = parts[0].astype(F32)
    for piece in [shift(parts[d], axis, d) for d in ORDER]:
        total = total + piece.astype(F32)
    return total.astype(BF16)


def regroup(k):
    pairs = []
    for x in range(4):
        for y in range(4):
            a = 2 * (x % 2) + y % 2
            pairs.append((4 * x + y, 4 * ((a + k) % 4) + x // 2 + 2 * (y // 2)))
    return pairs


def on_device(
    delta_query,
    delta_key,
    delta_value,
    delta_gate,
    write_strength,
    decay_log,
    kept_state,
    kept_kv,
    fresh_kv,
    attn_query,
    attn_gate,
    cached_len,
    slot_of_session,
    delta_out_weight,
    attn_out_weight,
):
    count = attn_query.shape[0]
    owners = 8
    owner_id = lax.axis_index(("z", "core"))
    x, y, core = lax.axis_index("x"), lax.axis_index("y"), lax.axis_index("core")
    session_ids = jnp.arange(slot_of_session.shape[0], dtype=jnp.int32)
    on_mine = slot_of_session // count == owner_id
    owner_of = session_ids // count
    wanted = on_mine[None, :] & (owner_of[None, :] == jnp.arange(owners, dtype=jnp.int32)[:, None])
    picked_slot = jnp.sum(jnp.where(wanted, slot_of_session[None, :] - owner_id * count, 0), axis=1)
    source = lax.dynamic_slice_in_dim(slot_of_session, owner_id * count, count) // count
    length = lax.dynamic_index_in_dim(cached_len, owner_id * count + x, 0, keepdims=False)
    source = source.astype(jnp.int32)

    kept_rows = kept_kv.transpose(0, 2, 1, 3).reshape(count, 128, 512)
    state_rows = kept_state.astype(BF16).reshape(count, 2, 4, 32, 128)
    state_rows = state_rows.transpose(0, 1, 3, 2, 4).reshape(count, 64, 512)
    leaving = jnp.take(jnp.concatenate([kept_rows, state_rows], axis=1), picked_slot, axis=0)
    landed = all_to_all(leaving, ("z", "core"))

    place = jnp.stack([2 * (x & 1) + (y & 1), core]).astype(jnp.int32)
    *blocks, delta_share = pack(
        after(place, leaving), attn_query, attn_gate, attn_out_weight, delta_out_weight
    )
    queries = [lax.ppermute(blocks[k], ("x", "y"), regroup(k)) for k in range(4)]

    delta_key = after(delta_key, leaving, *blocks)
    prepared = prep(delta_query, delta_key, delta_value, write_strength, decay_log)
    landed = after(landed, prepared)

    fresh_rows = fresh_kv.transpose(0, 2, 1, 3).reshape(count, 64, 512)
    chosen = select(source, landed, fresh_rows)
    rows = all_to_all(chosen, "x")
    delta_share = after(delta_share, chosen)
    delta_own = [delta_share] + [shift(delta_share, "y", d) for d in (1, 2, 3)]

    delta_heads, final_state = scan(after(source, chosen), landed, prepared, delta_gate)
    attn_own = stack_rows(queries, 1)
    rows = after(rows, delta_heads, attn_own)

    def swap_cores(array):
        return lax.ppermute(array, "core", [(0, 1), (1, 0)])

    attn_other = swap_cores(attn_own)

    def columns(target):
        return lax.dynamic_slice_in_dim(rows, (target & 1) * 256, 256, 2)

    parts = [columns(y + d) for d in range(4)]
    positions = [parts[0]] + [shift(parts[d], "y", d) for d in (1, 2, 3)]

    pieces = all_to_all(after(delta_heads, positions), "y")
    delta_own = stack_rows(after(delta_own, positions), 0)
    delta_other = swap_cores(delta_own)

    def quarters(first, second, *others):
        asked = jnp.stack([x, y, length, (y + first) & 3, (y + second) & 3, core])
        return attention(
            after(asked.astype(jnp.int32), *others), queries, positions, attn_own, attn_other
        )

    two, one = quarters(2, 1)
    scalars = jnp.stack([x, y, core]).astype(jnp.int32)
    delta_parts = delta_project(scalars, after(pieces, two), delta_own, delta_other)
    three, last = quarters(3, 0, delta_parts)
    delta_mixed = sum_over(delta_parts, "x")
    attn_mixed = sum_over([last, one, two, three], "y")
    return (delta_mixed, attn_mixed, final_state)


def solution(mesh):
    split = Mesh(np.asarray(mesh.devices).reshape(4, 2, 4, 4), ("z", "core", "x", "y"))
    cache, head = ("z", "core"), ("x", "y")
    in_specs = (
        P(cache, None, head),
        P(cache, None, head),
        P(cache, None, head),
        P(cache, None, head),
        P(cache, head, None),
        P(cache, head, None),
        P(cache, head, None, None),
        P(cache, head, None, None),
        P(cache, head, None, None),
        P(cache, None, head),
        P(cache, None, head),
        P(),
        P(),
        P(head, None),
        P(head, None),
    )
    out_specs = (
        P(cache + head, None),
        P(cache + head, None),
        P(cache, head, None, None),
    )
    return jax.shard_map(
        on_device, mesh=split, in_specs=in_specs, out_specs=out_specs, check_vma=False
    )
```

```python
import functools
import math

import jax
import jax.numpy as jnp
import numpy as np
from jax import lax
from jax.experimental import pallas as pl
from jax.experimental.pallas import tpu as pltpu
from jax.sharding import Mesh, PartitionSpec as P

F32 = jnp.float32
BF16 = jnp.bfloat16
CH = 128
HIGH = lax.Precision.HIGHEST
NEG = -1e30
VMEM = 60 * 1024 * 1024


def cost(us):
    return pl.CostEstimate(flops=int(us * 1e9), transcendentals=0, bytes_accessed=int(us * 3e6))


def after(value, *others):
    return lax.optimization_barrier((value, others))[0]


def mm(a, b):
    return lax.dot_general(a, b, (((1,), (0,)), ((), ())), preferred_element_type=F32)


def mm_nt(a, b, precision=None):
    return lax.dot_general(
        a, b, (((1,), (1,)), ((), ())), preferred_element_type=F32, precision=precision
    )


def prep_kernel(q_ref, k_ref, v_ref, b_ref, g_ref, wq_ref, u_ref, p_ref, kt_ref, dec_ref):
    row = lax.broadcasted_iota(jnp.int32, (CH, CH), 0)
    col = lax.broadcasted_iota(jnp.int32, (CH, CH), 1)
    strict = row > col
    incl = row >= col
    diag = row == col
    tri = jnp.where(incl, 1.0, 0.0).astype(F32)
    eye = jnp.where(diag, 1.0, 0.0).astype(F32)
    g8 = jnp.concatenate([g_ref[s] for s in range(4)], axis=0)
    b8 = jnp.concatenate([b_ref[s] for s in range(4)], axis=0)
    g_rows = mm_nt(g8, tri, HIGH)
    g_cols = mm_nt(tri, g8, HIGH)
    b_cols = mm_nt(eye, b8, HIGH)
    chains = []
    for s in range(4):
        k = k_ref[s]
        q = q_ref[s]
        kk = mm_nt(k, k)
        qk = mm_nt(q, k)
        kf = k.astype(F32)
        qf = q.astype(F32)
        rk = lax.rsqrt(jnp.sum(kf * kf, axis=1, keepdims=True) + 1e-6)
        rq = lax.rsqrt(jnp.sum(qf * qf, axis=1, keepdims=True) + 1e-6) * (1.0 / math.sqrt(128.0))
        rk_row = lax.rsqrt(jnp.sum(jnp.where(diag, kk, 0.0), axis=0, keepdims=True) + 1e-6)
        kkn = kk * rk * rk_row
        qkn = qk * rq * rk_row
        kn = kf * rk
        qn = qf * rq
        for h in range(2):
            i = 2 * s + h
            gc = g_cols[:, i : i + 1]
            gr = g_rows[i : i + 1, :]
            bc = b_cols[:, i : i + 1]
            decay = jnp.where(incl, jnp.exp(jnp.where(incl, gc - gr, 0.0)), 0.0)
            low = jnp.where(strict, decay * kkn * bc, 0.0)
            p_ref[0, i] = (decay * qkn).astype(BF16)
            growth = jnp.exp(gc)
            g_last = gr[:, CH - 1 : CH]
            tail = jnp.exp(g_last - gc)
            kt_ref[0, i] = (tail * kn).T.astype(BF16)
            wq_ref[0, i, CH:, :] = (growth * qn).astype(BF16)
            dec_ref[0, i : i + 1, :] = jnp.broadcast_to(jnp.exp(g_last), (1, CH))
            rhs = jnp.concatenate(
                [bc * v_ref[s, :, h * CH : (h + 1) * CH].astype(F32), (bc * growth) * kn], axis=1
            ).astype(BF16)
            chains.append([low, rhs])
    inverses = []
    pair = (row // 2 == col // 2) & strict
    for low, _ in chains:
        inverses.append(eye - jnp.where(pair, low, 0.0))
    m = 2
    while m < CH:
        mask = (row // (2 * m) == col // (2 * m)) & (row // m > col // m)
        lefts = [
            mm(jnp.where(mask, chains[i][0], 0.0).astype(BF16), inverses[i].astype(BF16))
            for i in range(8)
        ]
        steps = [mm(inverses[i].astype(BF16), lefts[i].astype(BF16)) for i in range(8)]
        inverses = [inverses[i] - steps[i] for i in range(8)]
        m *= 2
    for i in range(8):
        solved = mm(inverses[i].astype(BF16), chains[i][1])
        u_ref[0, i] = solved[:, :CH]
        wq_ref[0, i, :CH, :] = solved[:, CH:].astype(BF16)


def prep(delta_query, delta_key, delta_value, strengths, decays):
    chunks = delta_query.shape[1] // CH
    spec_tok = lambda w: pl.BlockSpec((4, CH, w), lambda c: (0, c, 0))
    spec_rate = pl.BlockSpec((4, 2, CH), lambda c: (0, 0, c))
    spec_out = lambda r: pl.BlockSpec((1, 8, r, CH), lambda c: (c, 0, 0, 0))
    shape = lambda r, t: jax.ShapeDtypeStruct((chunks, 8, r, CH), t)
    return pl.pallas_call(
        prep_kernel,
        grid=(chunks,),
        in_specs=[spec_tok(CH), spec_tok(CH), spec_tok(2 * CH), spec_rate, spec_rate],
        out_specs=[
            spec_out(2 * CH),
            spec_out(CH),
            spec_out(CH),
            spec_out(CH),
            pl.BlockSpec((1, 8, CH), lambda c: (c, 0, 0)),
        ],
        out_shape=[
            shape(2 * CH, BF16),
            shape(CH, F32),
            shape(CH, BF16),
            shape(CH, BF16),
            jax.ShapeDtypeStruct((chunks, 8, CH), F32),
        ],
        compiler_params=pltpu.CompilerParams(vmem_limit_bytes=VMEM),
        cost_estimate=cost(0.1),
        name="delta_prep",
    )(delta_query, delta_key, delta_value, strengths, decays)


def scan_kernel(
    src_ref, state_ref, wq_ref, u_ref, p_ref, kt_ref, dec_ref, gate_ref, heads_ref, final_ref, carry
):
    c = pl.program_id(0)

    @pl.when(c == 0)
    def _():
        for s in range(4):
            for h in range(2):
                for j in range(4):
                    block = state_ref[src_ref[s], 32 * h : 32 * h + 32, j * CH : (j + 1) * CH]
                    carry[2 * s + h, 32 * j : 32 * j + 32, :] = block.astype(F32)

    states = [carry[i] for i in range(8)]
    reads = [mm(wq_ref[0, i], states[i].astype(BF16)) for i in range(8)]
    updates = [(u_ref[0, i] - reads[i][:CH]).astype(BF16) for i in range(8)]
    for i in range(8):
        carry[i] = states[i] * dec_ref[0, i : i + 1, :] + mm(kt_ref[0, i], updates[i])
    for i in range(8):
        s, h = i // 2, i % 2
        out = reads[i][CH:] + mm(p_ref[0, i], updates[i])
        scale = lax.rsqrt(jnp.mean(out * out, axis=1, keepdims=True) + 1e-6)
        gate = gate_ref[s, :, h * CH : (h + 1) * CH].astype(F32)
        silu = gate / (1.0 + jnp.exp(-gate))
        heads_ref[0, s, :, h * CH : (h + 1) * CH] = (out * scale * silu).astype(BF16)

    @pl.when(c == pl.num_programs(0) - 1)
    def _():
        for s in range(4):
            for h in range(2):
                final_ref[s, h] = carry[2 * s + h]


def scan(source, arrived, prepared, delta_gate):
    wq, u0, p, kt, dec = prepared
    chunks = wq.shape[0]
    spec = lambda r: pl.BlockSpec((1, 8, r, CH), lambda c, *_: (c, 0, 0, 0))
    return pl.pallas_call(
        scan_kernel,
        grid_spec=pltpu.PrefetchScalarGridSpec(
            num_scalar_prefetch=1,
            grid=(chunks,),
            in_specs=[
                pl.BlockSpec((8, 64, 512), lambda c, *_: (0, 2, 0)),
                spec(2 * CH),
                spec(CH),
                spec(CH),
                spec(CH),
                pl.BlockSpec((1, 8, CH), lambda c, *_: (c, 0, 0)),
                pl.BlockSpec((4, CH, 2 * CH), lambda c, *_: (0, c, 0)),
            ],
            out_specs=[
                pl.BlockSpec((1, 4, CH, 2 * CH), lambda c, *_: (c, 0, 0, 0)),
                pl.BlockSpec((4, 2, CH, CH), lambda c, *_: (0, 0, 0, 0)),
            ],
            scratch_shapes=[pltpu.VMEM((8, CH, CH), F32)],
        ),
        out_shape=[
            jax.ShapeDtypeStruct((chunks, 4, CH, 2 * CH), BF16),
            jax.ShapeDtypeStruct((4, 2, CH, CH), F32),
        ],
        compiler_params=pltpu.CompilerParams(vmem_limit_bytes=VMEM),
        cost_estimate=cost(0.1),
        name="delta_scan",
    )(source, arrived, wq, u0, p, kt, dec, delta_gate)


def swap_halves(core, head):
    low, high = head[:, :CH], head[:, CH:]
    return jnp.concatenate(
        [jnp.where(core == 0, low, high), jnp.where(core == 0, high, low)], axis=1
    )


def delta_project_kernel(sc_ref, h0, h1, h2, h3, own_ref, other_ref, *outs):
    x, core = sc_ref[0], sc_ref[1]
    total = None
    for e, heads_ref in enumerate((h0, h1, h2, h3)):
        rows = jnp.concatenate([heads_ref[(x + d) & 3] for d in range(4)], axis=0)
        weight = jnp.concatenate([own_ref[e], other_ref[e]], axis=0)
        part = mm(swap_halves(core, rows), weight)
        total = part if total is None else total + part
    total = total.astype(BF16)
    for d, ref in enumerate(outs):
        ref[...] = total[d * CH : (d + 1) * CH]


def delta_project(scalars, pieces, own, other):
    weight = pl.BlockSpec((4, CH, 512), lambda i, sc: (0, i, 0))
    return pl.pallas_call(
        delta_project_kernel,
        grid_spec=pltpu.PrefetchScalarGridSpec(
            num_scalar_prefetch=1,
            grid=(4,),
            in_specs=[pl.BlockSpec((4, CH, 2 * CH), lambda i, sc: (0, 0, 0))] * 4 + [weight, weight],
            out_specs=[pl.BlockSpec((CH, 512), lambda i, sc: (0, i))] * 4,
        ),
        out_shape=[jax.ShapeDtypeStruct((CH, 2048), BF16)] * 4,
        compiler_params=pltpu.CompilerParams(vmem_limit_bytes=VMEM),
        cost_estimate=cost(0.1),
        name="delta_project",
    )(scalars, *pieces, own, other)


def pack_kernel(sc_ref, q_ref, g_ref, aw_ref, dw_ref, o0, o1, o2, o3, delta_ref):
    for k, out in enumerate((o0, o1, o2, o3)):
        j = (sc_ref[0] + k) & 3
        out[:512, :256] = q_ref[j]
        out[:512, 256:] = g_ref[j]
        for n in range(4):
            out[512 + n * 32 : 544 + n * 32] = aw_ref[:, n * 512 : (n + 1) * 512]
    for n in range(4):
        delta_ref[n * CH : (n + 1) * CH] = dw_ref[:, n * 512 : (n + 1) * 512]


def pack(scalars, query, gate, attn_weight, delta_weight):
    whole = pl.BlockSpec(query.shape, lambda i, sc: (0, 0, 0))
    return pl.pallas_call(
        pack_kernel,
        grid_spec=pltpu.PrefetchScalarGridSpec(
            num_scalar_prefetch=1,
            grid=(1,),
            in_specs=[
                whole,
                whole,
                pl.BlockSpec((32, 2048), lambda i, sc: (sc[1] * 4 + sc[2], 0)),
                pl.BlockSpec((CH, 2048), lambda i, sc: (sc[1], 0)),
            ],
            out_specs=[pl.BlockSpec((640, 512), lambda i, sc: (0, 0))] * 4
            + [pl.BlockSpec((512, 512), lambda i, sc: (0, 0))],
        ),
        out_shape=[jax.ShapeDtypeStruct((640, 512), BF16)] * 4
        + [jax.ShapeDtypeStruct((512, 512), BF16)],
        compiler_params=pltpu.CompilerParams(vmem_limit_bytes=VMEM),
        cost_estimate=cost(0.1),
        name="pack_queries",
    )(scalars, query, gate, attn_weight, delta_weight)


def stack_kernel(r0, r1, r2, r3, out):
    for k, ref in enumerate((r0, r1, r2, r3)):
        out[k] = ref[...]


def stack_rows(arrays, rows, block):
    return pl.pallas_call(
        stack_kernel,
        grid=(1,),
        in_specs=[pl.BlockSpec((rows, 512), lambda i: (block, 0))] * 4,
        out_specs=pl.BlockSpec((4, rows, 512), lambda i: (0, 0, 0)),
        out_shape=jax.ShapeDtypeStruct((4, rows, 512), BF16),
        compiler_params=pltpu.CompilerParams(vmem_limit_bytes=VMEM),
        cost_estimate=cost(0.1),
        name="stack_weights",
    )(*arrays)


def merge_kernel(sc_ref, r0, r1, r2, r3, out):
    for e, ref in enumerate((r0, r1, r2, r3)):
        at = ((sc_ref[0] - e) & 3) * 32
        for k in range(4):
            for n in range(4):
                rows = pl.ds(pl.multiple_of(n * CH + at, 32), 32)
                out[k, rows] = ref[k, n * 32 : (n + 1) * 32]


def merge_rows(z, arrays):
    vmem = pl.BlockSpec(memory_space=pltpu.VMEM)
    return pl.pallas_call(
        merge_kernel,
        in_specs=[pl.BlockSpec(memory_space=pltpu.SMEM)] + [vmem] * 4,
        out_specs=vmem,
        out_shape=jax.ShapeDtypeStruct((4, 512, 512), BF16),
        compiler_params=pltpu.CompilerParams(vmem_limit_bytes=VMEM),
        cost_estimate=cost(0.1),
        name="merge_weights",
    )(z, *arrays)


def select_kernel(src_ref, landed_ref, fresh_ref, out_ref):
    for j in range(4):
        out_ref[j, :CH] = landed_ref[src_ref[j], :CH]
        out_ref[j, CH:] = fresh_ref[j]


def select(source, landed, fresh):
    vmem = pl.BlockSpec(memory_space=pltpu.VMEM)
    return pl.pallas_call(
        select_kernel,
        in_specs=[pl.BlockSpec(memory_space=pltpu.SMEM), vmem, vmem],
        out_specs=vmem,
        out_shape=jax.ShapeDtypeStruct((4, CH + 64, 512), BF16),
        compiler_params=pltpu.CompilerParams(vmem_limit_bytes=VMEM),
        cost_estimate=cost(0.1),
        name="select_sessions",
    )(source, landed, fresh)


def attention_kernel(
    sc_ref, q0, q1, q2, q3, place_ref, own_hbm, other_hbm, o0, o1, w_ref, w_sem, keys, values, heads
):
    fetches = [
        pltpu.make_async_copy(hbm, w_ref.at[n], w_sem.at[n])
        for n, hbm in enumerate((own_hbm, other_hbm))
    ]
    for fetch in fetches:
        fetch.start()
    length = sc_ref[2]
    rows = 2 * CH
    at_kept = lax.broadcasted_iota(jnp.int32, (1, 256), 1)
    at_fresh = lax.broadcasted_iota(jnp.int32, (1, 128), 1)
    kept_bias, fresh_place = [], []
    for e in range(4):
        ref = place_ref.at[e]
        place = ((at_kept >> 6) * 4 + e) * 64 + (at_kept & 63)
        kept_bias.append(jnp.where(place < length, 0.0, NEG))
        fresh_place.append(((at_fresh >> 5) * 4 + e) * 32 + (at_fresh & 31))
        for j in range(4):
            kept_at, fresh_at = e * 256 + j * 64, 1024 + e * 128 + j * 32
            keys[kept_at : kept_at + 64] = ref[j, :64]
            values[kept_at : kept_at + 64] = ref[j, 64:128]
            keys[fresh_at : fresh_at + 32] = ref[j, 128:160]
            values[fresh_at : fresh_at + 32] = ref[j, 160:]
    kept_bias = jnp.concatenate(kept_bias, axis=1)
    fresh_place = jnp.concatenate(fresh_place, axis=1)
    token = lax.broadcasted_iota(jnp.int32, (rows, 512), 0) & (CH - 1)
    scale = math.log2(math.e) / 16.0

    def load(n, pair, cols):
        at = pl.ds(pl.multiple_of(sc_ref[3 + n] * CH, CH), CH)
        return jnp.concatenate([r[at, cols] for r in pair], axis=0)

    def score(n, pair):
        query = load(n, pair, slice(0, 256))
        return mm_nt(query, keys[:1024]), mm_nt(query, keys[1024:])

    groups = [(n, g) for n in range(2) for g in range(2)]
    pairs = ((q0, q1), (q2, q3))
    ahead = score(0, pairs[0])
    for step, (n, g) in enumerate(groups):
        kept, fresh = ahead
        if step + 1 < len(groups):
            ahead = score(groups[step + 1][0], pairs[groups[step + 1][1]])
        kept = kept + kept_bias
        fresh = jnp.where(fresh_place <= token + sc_ref[3 + n] * CH, fresh, NEG)
        peak = jnp.maximum(
            jnp.max(kept, axis=1, keepdims=True), jnp.max(fresh, axis=1, keepdims=True)
        )
        kept = jnp.exp2((kept - peak) * scale)
        fresh = jnp.exp2((fresh - peak) * scale)
        total = jnp.sum(kept, axis=1, keepdims=True) + jnp.sum(fresh, axis=1, keepdims=True)
        mixed = mm(kept.astype(BF16), values[:1024]) + mm(fresh.astype(BF16), values[1024:])
        gate = load(n, pairs[g], slice(256, 512)).astype(F32)
        gated = (mixed / (total * (1.0 + jnp.exp(-gate)))).astype(BF16)
        for i in range(2):
            k = 2 * g + i
            heads[n * CH : (n + 1) * CH, k * 256 : (k + 1) * 256] = gated[i * CH : (i + 1) * CH]
    for fetch in fetches:
        fetch.wait()
    gated = [swap_halves(sc_ref[5], heads[:, k * 256 : (k + 1) * 256]) for k in range(4)]
    for j in range(4):
        rows = slice(j * CH, (j + 1) * CH)
        out = sum(
            mm(gated[k], jnp.concatenate([w_ref[0, k, rows], w_ref[1, k, rows]], axis=0))
            for k in range(4)
        ).astype(BF16)
        o0[:, j * 512 : (j + 1) * 512] = out[:CH]
        o1[:, j * 512 : (j + 1) * 512] = out[CH:]


def attention(scalars, queries, positions, own, other):
    whole = lambda a: pl.BlockSpec(a.shape, lambda i, sc: (0,) * a.ndim)
    return pl.pallas_call(
        attention_kernel,
        grid_spec=pltpu.PrefetchScalarGridSpec(
            num_scalar_prefetch=1,
            grid=(1,),
            in_specs=[pl.BlockSpec((512, 512), lambda i, sc: (0, 0))] * 4
            + [whole(positions)]
            + [pl.BlockSpec(memory_space=pl.ANY)] * 2,
            out_specs=[pl.BlockSpec((CH, 2048), lambda i, sc: (0, 0))] * 2,
            scratch_shapes=[
                pltpu.VMEM((2, 4, 512, 512), BF16),
                pltpu.SemaphoreType.DMA((2,)),
                pltpu.VMEM((1536, 256), BF16),
                pltpu.VMEM((1536, 256), BF16),
                pltpu.VMEM((2 * CH, 1024), BF16),
            ],
        ),
        out_shape=[jax.ShapeDtypeStruct((CH, 2048), BF16)] * 2,
        compiler_params=pltpu.CompilerParams(vmem_limit_bytes=VMEM),
        cost_estimate=cost(0.1),
        name="attention_project",
    )(scalars, *queries, positions, own, other)


ORDER = (2, 1, 3)


def shift(array, axis, by):
    return lax.ppermute(array, axis, [(i, (i + by) % 4) for i in range(4)])


def row_of(array, index):
    return lax.dynamic_index_in_dim(array, index, 0, keepdims=False)


def all_to_all(array, axis):
    return lax.all_to_all(array, axis, split_axis=0, concat_axis=0, tiled=True)


def sum_over(parts, axis):
    total = parts[0].astype(F32)
    for piece in [shift(parts[d], axis, d) for d in ORDER]:
        total = total + piece.astype(F32)
    return total.astype(BF16)


def regroup(k):
    pairs = []
    for x in range(4):
        for y in range(4):
            a = 2 * (x % 2) + y % 2
            pairs.append((4 * x + y, 4 * ((a + k) % 4) + x // 2 + 2 * (y // 2)))
    return pairs


def on_device(
    delta_query,
    delta_key,
    delta_value,
    delta_gate,
    write_strength,
    decay_log,
    kept_state,
    kept_kv,
    fresh_kv,
    attn_query,
    attn_gate,
    cached_len,
    slot_of_session,
    delta_out_weight,
    attn_out_weight,
):
    count = attn_query.shape[0]
    owners = 8
    owner_id = lax.axis_index(("z", "core"))
    x, y, core = lax.axis_index("x"), lax.axis_index("y"), lax.axis_index("core")
    session_ids = jnp.arange(slot_of_session.shape[0], dtype=jnp.int32)
    on_mine = slot_of_session // count == owner_id
    owner_of = session_ids // count
    wanted = on_mine[None, :] & (owner_of[None, :] == jnp.arange(owners, dtype=jnp.int32)[:, None])
    picked_slot = jnp.sum(jnp.where(wanted, slot_of_session[None, :] - owner_id * count, 0), axis=1)
    source = lax.dynamic_slice_in_dim(slot_of_session, owner_id * count, count) // count
    length = lax.dynamic_index_in_dim(cached_len, owner_id * count + x, 0, keepdims=False)
    source = source.astype(jnp.int32)

    kept_rows = kept_kv.transpose(0, 2, 1, 3).reshape(count, 128, 512)
    state_rows = kept_state.astype(BF16).reshape(count, 2, 4, 32, 128)
    state_rows = state_rows.transpose(0, 1, 3, 2, 4).reshape(count, 64, 512)
    leaving = jnp.take(jnp.concatenate([kept_rows, state_rows], axis=1), picked_slot, axis=0)
    landed = all_to_all(leaving, ("z", "core"))

    z = lax.axis_index("z").astype(jnp.int32)
    place = jnp.stack([2 * (x & 1) + (y & 1), core, z]).astype(jnp.int32)
    *blocks, delta_share = pack(
        after(place, leaving), attn_query, attn_gate, attn_out_weight, delta_out_weight
    )
    def regrouped(array, k):
        return lax.ppermute(array, ("x", "y"), regroup(k))

    def swap_cores(array):
        return lax.ppermute(array, "core", [(0, 1), (1, 0)])

    delta_own = [delta_share] + [shift(delta_share, "y", d) for d in (1, 2, 3)]

    delta_key = after(delta_key, *blocks)
    prepared = prep(delta_query, delta_key, delta_value, write_strength, decay_log)
    landed = after(landed, prepared, *delta_own)
    queries = [regrouped(block, k) for k, block in zip((0, 1), after(blocks[:2], prepared))]

    fresh_rows = fresh_kv.transpose(0, 2, 1, 3).reshape(count, 64, 512)
    chosen = select(source, landed, fresh_rows)
    rows = all_to_all(chosen, "x")
    queries += [regrouped(block, k) for k, block in zip((2, 3), after(blocks[2:], chosen))]

    delta_heads, final_state = scan(after(source, chosen, *queries[:2]), landed, prepared, delta_gate)
    quarter = [row_of(delta_heads, (y + d) & 3) for d in range(4)]
    pieces = [quarter[0]] + [shift(quarter[d], "y", d) for d in (1, 2, 3)]
    rows = after(rows, *queries, *pieces)

    low, high = rows[:, :, :256], rows[:, :, 256:]
    leaving = jnp.stack([low, high, low, high], axis=0)
    positions = all_to_all(leaving, "y")

    eighths = stack_rows(after(queries, leaving), CH, 4)
    eighths = [eighths] + [shift(eighths, "z", d) for d in (1, 2, 3)]
    delta_own = stack_rows(after(delta_own, leaving), 512, 0)
    delta_other = swap_cores(delta_own)
    scalars = jnp.stack([x, core]).astype(jnp.int32)
    delta_parts = delta_project(scalars, after(pieces, positions), delta_own, delta_other)
    attn_own = merge_rows(z[None], after(eighths, delta_parts))
    attn_other = swap_cores(attn_own)
    positions = after(positions, delta_parts)

    def quarters(first, second, *others):
        asked = jnp.stack([x, y, length, (y + first) & 3, (y + second) & 3, core])
        return attention(
            after(asked.astype(jnp.int32), *others), queries, positions, attn_own, attn_other
        )

    two, one = quarters(2, 1)
    three, last = quarters(3, 0, two)
    delta_mixed = sum_over(delta_parts, "x")
    attn_mixed = sum_over([last, one, two, three], "y")
    return (delta_mixed, attn_mixed, final_state)


def solution(mesh):
    split = Mesh(np.asarray(mesh.devices).reshape(4, 2, 4, 4), ("z", "core", "x", "y"))
    cache, head = ("z", "core"), ("x", "y")
    in_specs = (
        P(cache, None, head),
        P(cache, None, head),
        P(cache, None, head),
        P(cache, None, head),
        P(cache, head, None),
        P(cache, head, None),
        P(cache, head, None, None),
        P(cache, head, None, None),
        P(cache, head, None, None),
        P(cache, None, head),
        P(cache, None, head),
        P(),
        P(),
        P(head, None),
        P(head, None),
    )
    out_specs = (
        P(cache + head, None),
        P(cache + head, None),
        P(cache, head, None, None),
    )
    return jax.shard_map(
        on_device, mesh=split, in_specs=in_specs, out_specs=out_specs, check_vma=False
    )
```

```python
import functools
import math

import jax
import jax.numpy as jnp
import numpy as np
from jax import lax
from jax.experimental import pallas as pl
from jax.experimental.pallas import tpu as pltpu
from jax.sharding import Mesh, PartitionSpec as P

F32 = jnp.float32
BF16 = jnp.bfloat16
CH = 128
HIGH = lax.Precision.HIGHEST
NEG = -1e30
VMEM = 60 * 1024 * 1024


def cost(us):
    return pl.CostEstimate(flops=int(us * 1e9), transcendentals=0, bytes_accessed=int(us * 3e6))


def after(value, *others):
    return lax.optimization_barrier((value, others))[0]


def mm(a, b):
    return lax.dot_general(a, b, (((1,), (0,)), ((), ())), preferred_element_type=F32)


def mm_nt(a, b, precision=None):
    return lax.dot_general(
        a, b, (((1,), (1,)), ((), ())), preferred_element_type=F32, precision=precision
    )


def prep_kernel(q_ref, k_ref, v_ref, b_ref, g_ref, wq_ref, u_ref, p_ref, kt_ref, dec_ref):
    row = lax.broadcasted_iota(jnp.int32, (CH, CH), 0)
    col = lax.broadcasted_iota(jnp.int32, (CH, CH), 1)
    strict = row > col
    incl = row >= col
    diag = row == col
    tri = jnp.where(incl, 1.0, 0.0).astype(F32)
    eye = jnp.where(diag, 1.0, 0.0).astype(F32)
    g8 = jnp.concatenate([g_ref[s] for s in range(4)], axis=0)
    b8 = jnp.concatenate([b_ref[s] for s in range(4)], axis=0)
    g_rows = mm_nt(g8, tri, HIGH)
    g_cols = mm_nt(tri, g8, HIGH)
    b_cols = mm_nt(eye, b8, HIGH)
    chains = []
    for s in range(4):
        k = k_ref[s]
        q = q_ref[s]
        kk = mm_nt(k, k)
        qk = mm_nt(q, k)
        kf = k.astype(F32)
        qf = q.astype(F32)
        rk = lax.rsqrt(jnp.sum(kf * kf, axis=1, keepdims=True) + 1e-6)
        rq = lax.rsqrt(jnp.sum(qf * qf, axis=1, keepdims=True) + 1e-6) * (1.0 / math.sqrt(128.0))
        rk_row = lax.rsqrt(jnp.sum(jnp.where(diag, kk, 0.0), axis=0, keepdims=True) + 1e-6)
        kkn = kk * rk * rk_row
        qkn = qk * rq * rk_row
        kn = kf * rk
        qn = qf * rq
        for h in range(2):
            i = 2 * s + h
            gc = g_cols[:, i : i + 1]
            gr = g_rows[i : i + 1, :]
            bc = b_cols[:, i : i + 1]
            decay = jnp.where(incl, jnp.exp(jnp.where(incl, gc - gr, 0.0)), 0.0)
            low = jnp.where(strict, decay * kkn * bc, 0.0)
            p_ref[0, i] = (decay * qkn).astype(BF16)
            growth = jnp.exp(gc)
            g_last = gr[:, CH - 1 : CH]
            tail = jnp.exp(g_last - gc)
            kt_ref[0, i] = (tail * kn).T.astype(BF16)
            wq_ref[0, i, CH:, :] = (growth * qn).astype(BF16)
            dec_ref[0, i : i + 1, :] = jnp.broadcast_to(jnp.exp(g_last), (1, CH))
            rhs = jnp.concatenate(
                [bc * v_ref[s, :, h * CH : (h + 1) * CH].astype(F32), (bc * growth) * kn], axis=1
            ).astype(BF16)
            chains.append([low, rhs])
    inverses = []
    pair = (row // 2 == col // 2) & strict
    for low, _ in chains:
        inverses.append(eye - jnp.where(pair, low, 0.0))
    m = 2
    while m < CH:
        mask = (row // (2 * m) == col // (2 * m)) & (row // m > col // m)
        lefts = [
            mm(jnp.where(mask, chains[i][0], 0.0).astype(BF16), inverses[i].astype(BF16))
            for i in range(8)
        ]
        steps = [mm(inverses[i].astype(BF16), lefts[i].astype(BF16)) for i in range(8)]
        inverses = [inverses[i] - steps[i] for i in range(8)]
        m *= 2
    for i in range(8):
        solved = mm(inverses[i].astype(BF16), chains[i][1])
        u_ref[0, i] = solved[:, :CH]
        wq_ref[0, i, :CH, :] = solved[:, CH:].astype(BF16)


def prep(delta_query, delta_key, delta_value, strengths, decays):
    chunks = delta_query.shape[1] // CH
    spec_tok = lambda w: pl.BlockSpec((4, CH, w), lambda c: (0, c, 0))
    spec_rate = pl.BlockSpec((4, 2, CH), lambda c: (0, 0, c))
    spec_out = lambda r: pl.BlockSpec((1, 8, r, CH), lambda c: (c, 0, 0, 0))
    shape = lambda r, t: jax.ShapeDtypeStruct((chunks, 8, r, CH), t)
    return pl.pallas_call(
        prep_kernel,
        grid=(chunks,),
        in_specs=[spec_tok(CH), spec_tok(CH), spec_tok(2 * CH), spec_rate, spec_rate],
        out_specs=[
            spec_out(2 * CH),
            spec_out(CH),
            spec_out(CH),
            spec_out(CH),
            pl.BlockSpec((1, 8, CH), lambda c: (c, 0, 0)),
        ],
        out_shape=[
            shape(2 * CH, BF16),
            shape(CH, F32),
            shape(CH, BF16),
            shape(CH, BF16),
            jax.ShapeDtypeStruct((chunks, 8, CH), F32),
        ],
        compiler_params=pltpu.CompilerParams(vmem_limit_bytes=VMEM),
        cost_estimate=cost(0.1),
        name="delta_prep",
    )(delta_query, delta_key, delta_value, strengths, decays)


def scan_kernel(
    src_ref, state_ref, wq_ref, u_ref, p_ref, kt_ref, dec_ref, gate_ref, heads_ref, final_ref, carry
):
    c = pl.program_id(0)

    @pl.when(c == 0)
    def _():
        for s in range(4):
            for h in range(2):
                for j in range(4):
                    block = state_ref[src_ref[s], 32 * h : 32 * h + 32, j * CH : (j + 1) * CH]
                    carry[2 * s + h, 32 * j : 32 * j + 32, :] = block.astype(F32)

    states = [carry[i] for i in range(8)]
    reads = [mm(wq_ref[0, i], states[i].astype(BF16)) for i in range(8)]
    updates = [(u_ref[0, i] - reads[i][:CH]).astype(BF16) for i in range(8)]
    for i in range(8):
        carry[i] = states[i] * dec_ref[0, i : i + 1, :] + mm(kt_ref[0, i], updates[i])
    for i in range(8):
        s, h = i // 2, i % 2
        out = reads[i][CH:] + mm(p_ref[0, i], updates[i])
        scale = lax.rsqrt(jnp.mean(out * out, axis=1, keepdims=True) + 1e-6)
        gate = gate_ref[s, :, h * CH : (h + 1) * CH].astype(F32)
        silu = gate / (1.0 + jnp.exp(-gate))
        heads_ref[0, s, :, h * CH : (h + 1) * CH] = (out * scale * silu).astype(BF16)

    @pl.when(c == pl.num_programs(0) - 1)
    def _():
        for s in range(4):
            for h in range(2):
                final_ref[s, h] = carry[2 * s + h]


def scan(source, arrived, prepared, delta_gate):
    wq, u0, p, kt, dec = prepared
    chunks = wq.shape[0]
    spec = lambda r: pl.BlockSpec((1, 8, r, CH), lambda c, *_: (c, 0, 0, 0))
    return pl.pallas_call(
        scan_kernel,
        grid_spec=pltpu.PrefetchScalarGridSpec(
            num_scalar_prefetch=1,
            grid=(chunks,),
            in_specs=[
                pl.BlockSpec((8, 64, 512), lambda c, *_: (0, 2, 0)),
                spec(2 * CH),
                spec(CH),
                spec(CH),
                spec(CH),
                pl.BlockSpec((1, 8, CH), lambda c, *_: (c, 0, 0)),
                pl.BlockSpec((4, CH, 2 * CH), lambda c, *_: (0, c, 0)),
            ],
            out_specs=[
                pl.BlockSpec((1, 4, CH, 2 * CH), lambda c, *_: (c, 0, 0, 0)),
                pl.BlockSpec((4, 2, CH, CH), lambda c, *_: (0, 0, 0, 0)),
            ],
            scratch_shapes=[pltpu.VMEM((8, CH, CH), F32)],
        ),
        out_shape=[
            jax.ShapeDtypeStruct((chunks, 4, CH, 2 * CH), BF16),
            jax.ShapeDtypeStruct((4, 2, CH, CH), F32),
        ],
        compiler_params=pltpu.CompilerParams(vmem_limit_bytes=VMEM),
        cost_estimate=cost(0.1),
        name="delta_scan",
    )(source, arrived, wq, u0, p, kt, dec, delta_gate)


def swap_halves(core, head):
    low, high = head[:, :CH], head[:, CH:]
    return jnp.concatenate(
        [jnp.where(core == 0, low, high), jnp.where(core == 0, high, low)], axis=1
    )


def delta_project_kernel(sc_ref, h0, h1, h2, h3, own_ref, other_ref, *outs):
    x, core = sc_ref[0], sc_ref[1]
    total = None
    for e, heads_ref in enumerate((h0, h1, h2, h3)):
        rows = jnp.concatenate([heads_ref[(x + d) & 3] for d in range(4)], axis=0)
        weight = jnp.concatenate([own_ref[e], other_ref[e]], axis=0)
        part = mm(swap_halves(core, rows), weight)
        total = part if total is None else total + part
    total = total.astype(BF16)
    for d, ref in enumerate(outs):
        ref[...] = total[d * CH : (d + 1) * CH]


def delta_project(scalars, pieces, own, other):
    weight = pl.BlockSpec((4, CH, 512), lambda i, sc: (0, i, 0))
    return pl.pallas_call(
        delta_project_kernel,
        grid_spec=pltpu.PrefetchScalarGridSpec(
            num_scalar_prefetch=1,
            grid=(4,),
            in_specs=[pl.BlockSpec((4, CH, 2 * CH), lambda i, sc: (0, 0, 0))] * 4 + [weight, weight],
            out_specs=[pl.BlockSpec((CH, 512), lambda i, sc: (0, i))] * 4,
        ),
        out_shape=[jax.ShapeDtypeStruct((CH, 2048), BF16)] * 4,
        compiler_params=pltpu.CompilerParams(vmem_limit_bytes=VMEM),
        cost_estimate=cost(0.1),
        name="delta_project",
    )(scalars, *pieces, own, other)


def pack_kernel(sc_ref, q_ref, g_ref, aw_ref, dw_ref, o0, o1, o2, o3, delta_ref):
    for k, out in enumerate((o0, o1, o2, o3)):
        j = (sc_ref[0] + k) & 3
        out[:512, :256] = q_ref[j]
        out[:512, 256:] = g_ref[j]
        for n in range(4):
            out[512 + n * 32 : 544 + n * 32] = aw_ref[:, n * 512 : (n + 1) * 512]
    for n in range(4):
        delta_ref[n * CH : (n + 1) * CH] = dw_ref[:, n * 512 : (n + 1) * 512]


def pack(scalars, query, gate, attn_weight, delta_weight):
    whole = pl.BlockSpec(query.shape, lambda i, sc: (0, 0, 0))
    return pl.pallas_call(
        pack_kernel,
        grid_spec=pltpu.PrefetchScalarGridSpec(
            num_scalar_prefetch=1,
            grid=(1,),
            in_specs=[
                whole,
                whole,
                pl.BlockSpec((32, 2048), lambda i, sc: (sc[1] * 4 + sc[2], 0)),
                pl.BlockSpec((CH, 2048), lambda i, sc: (sc[1], 0)),
            ],
            out_specs=[pl.BlockSpec((640, 512), lambda i, sc: (0, 0))] * 4
            + [pl.BlockSpec((512, 512), lambda i, sc: (0, 0))],
        ),
        out_shape=[jax.ShapeDtypeStruct((640, 512), BF16)] * 4
        + [jax.ShapeDtypeStruct((512, 512), BF16)],
        compiler_params=pltpu.CompilerParams(vmem_limit_bytes=VMEM),
        cost_estimate=cost(0.1),
        name="pack_queries",
    )(scalars, query, gate, attn_weight, delta_weight)


def stack_kernel(r0, r1, r2, r3, out):
    for k, ref in enumerate((r0, r1, r2, r3)):
        out[k] = ref[...]


def stack_rows(arrays, rows, block):
    return pl.pallas_call(
        stack_kernel,
        grid=(1,),
        in_specs=[pl.BlockSpec((rows, 512), lambda i: (block, 0))] * 4,
        out_specs=pl.BlockSpec((4, rows, 512), lambda i: (0, 0, 0)),
        out_shape=jax.ShapeDtypeStruct((4, rows, 512), BF16),
        compiler_params=pltpu.CompilerParams(vmem_limit_bytes=VMEM),
        cost_estimate=cost(0.1),
        name="stack_weights",
    )(*arrays)


def merge_kernel(sc_ref, r0, r1, r2, r3, out):
    for e, ref in enumerate((r0, r1, r2, r3)):
        at = ((sc_ref[0] - e) & 3) * 32
        for k in range(4):
            for n in range(4):
                rows = pl.ds(pl.multiple_of(n * CH + at, 32), 32)
                out[k, rows] = ref[k, n * 32 : (n + 1) * 32]


def merge_rows(z, arrays):
    vmem = pl.BlockSpec(memory_space=pltpu.VMEM)
    return pl.pallas_call(
        merge_kernel,
        in_specs=[pl.BlockSpec(memory_space=pltpu.SMEM)] + [vmem] * 4,
        out_specs=vmem,
        out_shape=jax.ShapeDtypeStruct((4, 512, 512), BF16),
        compiler_params=pltpu.CompilerParams(vmem_limit_bytes=VMEM),
        cost_estimate=cost(0.1),
        name="merge_weights",
    )(z, *arrays)


def select_kernel(src_ref, landed_ref, fresh_ref, out_ref):
    for j in range(4):
        out_ref[j, :CH] = landed_ref[src_ref[j], :CH]
        out_ref[j, CH:] = fresh_ref[j]


def select(source, landed, fresh):
    vmem = pl.BlockSpec(memory_space=pltpu.VMEM)
    return pl.pallas_call(
        select_kernel,
        in_specs=[pl.BlockSpec(memory_space=pltpu.SMEM), vmem, vmem],
        out_specs=vmem,
        out_shape=jax.ShapeDtypeStruct((4, CH + 64, 512), BF16),
        compiler_params=pltpu.CompilerParams(vmem_limit_bytes=VMEM),
        cost_estimate=cost(0.1),
        name="select_sessions",
    )(source, landed, fresh)


def attention_kernel(
    sc_ref, q0, q1, q2, q3, place_ref, own_hbm, other_hbm, o0, o1, w_ref, w_sem, keys, values, heads
):
    fetches = [
        pltpu.make_async_copy(hbm, w_ref.at[n], w_sem.at[n])
        for n, hbm in enumerate((own_hbm, other_hbm))
    ]
    for fetch in fetches:
        fetch.start()
    length = sc_ref[2]
    rows = 2 * CH
    at_kept = lax.broadcasted_iota(jnp.int32, (1, 256), 1)
    at_fresh = lax.broadcasted_iota(jnp.int32, (1, 128), 1)
    kept_bias, fresh_place = [], []
    for e in range(4):
        ref = place_ref.at[e]
        place = ((at_kept >> 6) * 4 + e) * 64 + (at_kept & 63)
        kept_bias.append(jnp.where(place < length, 0.0, NEG))
        fresh_place.append(((at_fresh >> 5) * 4 + e) * 32 + (at_fresh & 31))
        for j in range(4):
            kept_at, fresh_at = e * 256 + j * 64, 1024 + e * 128 + j * 32
            keys[kept_at : kept_at + 64] = ref[j, :64]
            values[kept_at : kept_at + 64] = ref[j, 64:128]
            keys[fresh_at : fresh_at + 32] = ref[j, 128:160]
            values[fresh_at : fresh_at + 32] = ref[j, 160:]
    kept_bias = jnp.concatenate(kept_bias, axis=1)
    fresh_place = jnp.concatenate(fresh_place, axis=1)
    token = lax.broadcasted_iota(jnp.int32, (rows, 512), 0) & (CH - 1)
    scale = math.log2(math.e) / 16.0

    def load(n, pair, cols):
        at = pl.ds(pl.multiple_of(sc_ref[3 + n] * CH, CH), CH)
        return jnp.concatenate([r[at, cols] for r in pair], axis=0)

    def score(n, pair):
        query = load(n, pair, slice(0, 256))
        return mm_nt(query, keys[:1024]), mm_nt(query, keys[1024:])

    groups = [(n, g) for n in range(2) for g in range(2)]
    pairs = ((q0, q1), (q2, q3))
    ahead = score(0, pairs[0])
    for step, (n, g) in enumerate(groups):
        kept, fresh = ahead
        if step + 1 < len(groups):
            ahead = score(groups[step + 1][0], pairs[groups[step + 1][1]])
        kept = kept + kept_bias
        fresh = jnp.where(fresh_place <= token + sc_ref[3 + n] * CH, fresh, NEG)
        peak = jnp.maximum(
            jnp.max(kept, axis=1, keepdims=True), jnp.max(fresh, axis=1, keepdims=True)
        )
        kept = jnp.exp2((kept - peak) * scale)
        fresh = jnp.exp2((fresh - peak) * scale)
        total = jnp.sum(kept, axis=1, keepdims=True) + jnp.sum(fresh, axis=1, keepdims=True)
        mixed = mm(kept.astype(BF16), values[:1024]) + mm(fresh.astype(BF16), values[1024:])
        gate = load(n, pairs[g], slice(256, 512)).astype(F32)
        gated = (mixed / (total * (1.0 + jnp.exp(-gate)))).astype(BF16)
        for i in range(2):
            k = 2 * g + i
            heads[n * CH : (n + 1) * CH, k * 256 : (k + 1) * 256] = gated[i * CH : (i + 1) * CH]
    for fetch in fetches:
        fetch.wait()
    gated = [swap_halves(sc_ref[5], heads[:, k * 256 : (k + 1) * 256]) for k in range(4)]
    for j in range(4):
        rows = slice(j * CH, (j + 1) * CH)
        out = sum(
            mm(gated[k], jnp.concatenate([w_ref[0, k, rows], w_ref[1, k, rows]], axis=0))
            for k in range(4)
        ).astype(BF16)
        o0[:, j * 512 : (j + 1) * 512] = out[:CH]
        o1[:, j * 512 : (j + 1) * 512] = out[CH:]


def attention(scalars, queries, positions, own, other):
    whole = lambda a: pl.BlockSpec(a.shape, lambda i, sc: (0,) * a.ndim)
    return pl.pallas_call(
        attention_kernel,
        grid_spec=pltpu.PrefetchScalarGridSpec(
            num_scalar_prefetch=1,
            grid=(1,),
            in_specs=[pl.BlockSpec((512, 512), lambda i, sc: (0, 0))] * 4
            + [whole(positions)]
            + [pl.BlockSpec(memory_space=pl.ANY)] * 2,
            out_specs=[pl.BlockSpec((CH, 2048), lambda i, sc: (0, 0))] * 2,
            scratch_shapes=[
                pltpu.VMEM((2, 4, 512, 512), BF16),
                pltpu.SemaphoreType.DMA((2,)),
                pltpu.VMEM((1536, 256), BF16),
                pltpu.VMEM((1536, 256), BF16),
                pltpu.VMEM((2 * CH, 1024), BF16),
            ],
        ),
        out_shape=[jax.ShapeDtypeStruct((CH, 2048), BF16)] * 2,
        compiler_params=pltpu.CompilerParams(vmem_limit_bytes=VMEM),
        cost_estimate=cost(0.1),
        name="attention_project",
    )(scalars, *queries, positions, own, other)


ORDER = (2, 1, 3)


def shift(array, axis, by):
    return lax.ppermute(array, axis, [(i, (i + by) % 4) for i in range(4)])


def row_of(array, index):
    return lax.dynamic_index_in_dim(array, index, 0, keepdims=False)


def all_to_all(array, axis):
    return lax.all_to_all(array, axis, split_axis=0, concat_axis=0, tiled=True)


def sum_over(parts, axis):
    total = parts[0].astype(F32)
    for piece in [shift(parts[d], axis, d) for d in ORDER]:
        total = total + piece.astype(F32)
    return total.astype(BF16)


def regroup(k):
    pairs = []
    for x in range(4):
        for y in range(4):
            a = 2 * (x % 2) + y % 2
            pairs.append((4 * x + y, 4 * ((a + k) % 4) + x // 2 + 2 * (y // 2)))
    return pairs


def on_device(
    delta_query,
    delta_key,
    delta_value,
    delta_gate,
    write_strength,
    decay_log,
    kept_state,
    kept_kv,
    fresh_kv,
    attn_query,
    attn_gate,
    cached_len,
    slot_of_session,
    delta_out_weight,
    attn_out_weight,
):
    count = attn_query.shape[0]
    owners = 8
    owner_id = lax.axis_index(("z", "core"))
    x, y, core = lax.axis_index("x"), lax.axis_index("y"), lax.axis_index("core")
    session_ids = jnp.arange(slot_of_session.shape[0], dtype=jnp.int32)
    on_mine = slot_of_session // count == owner_id
    owner_of = session_ids // count
    wanted = on_mine[None, :] & (owner_of[None, :] == jnp.arange(owners, dtype=jnp.int32)[:, None])
    picked_slot = jnp.sum(jnp.where(wanted, slot_of_session[None, :] - owner_id * count, 0), axis=1)
    source = lax.dynamic_slice_in_dim(slot_of_session, owner_id * count, count) // count
    length = lax.dynamic_index_in_dim(cached_len, owner_id * count + x, 0, keepdims=False)
    source = source.astype(jnp.int32)

    kept_rows = kept_kv.transpose(0, 2, 1, 3).reshape(count, 128, 512)
    state_rows = kept_state.astype(BF16).reshape(count, 2, 4, 32, 128)
    state_rows = state_rows.transpose(0, 1, 3, 2, 4).reshape(count, 64, 512)
    leaving = jnp.take(jnp.concatenate([kept_rows, state_rows], axis=1), picked_slot, axis=0)
    landed = all_to_all(leaving, ("z", "core"))

    z = lax.axis_index("z").astype(jnp.int32)
    place = jnp.stack([2 * (x & 1) + (y & 1), core, z]).astype(jnp.int32)
    *blocks, delta_share = pack(
        after(place, leaving), attn_query, attn_gate, attn_out_weight, delta_out_weight
    )
    def regrouped(array, k):
        return lax.ppermute(array, ("x", "y"), regroup(k))

    def swap_cores(array):
        return lax.ppermute(array, "core", [(0, 1), (1, 0)])

    queries = [regrouped(blocks[k], k) for k in range(4)]

    fresh_rows = fresh_kv.transpose(0, 2, 1, 3).reshape(count, 64, 512)
    landed = after(landed, *blocks)
    chosen = select(source, landed, fresh_rows)
    rows = all_to_all(chosen, "x")
    delta_share = after(delta_share, chosen)
    delta_own = [delta_share] + [shift(delta_share, "y", d) for d in (1, 2, 3)]

    delta_key = after(delta_key, chosen)
    prepared = prep(delta_query, delta_key, delta_value, write_strength, decay_log)
    delta_heads, final_state = scan(source, landed, prepared, delta_gate)
    quarter = [row_of(delta_heads, (y + d) & 3) for d in range(4)]
    pieces = [quarter[0]] + [shift(quarter[d], "y", d) for d in (1, 2, 3)]
    rows = after(rows, delta_heads, *queries)

    low, high = rows[:, :, :256], rows[:, :, 256:]
    leaving = jnp.stack([low, high, low, high], axis=0)
    positions = all_to_all(leaving, "y")

    eighths = stack_rows(after(queries, leaving), CH, 4)
    eighths = [eighths] + [shift(eighths, "z", d) for d in (1, 2, 3)]
    delta_own = stack_rows(after(delta_own, positions), 512, 0)
    delta_other = swap_cores(delta_own)
    scalars = jnp.stack([x, core]).astype(jnp.int32)
    attn_own = merge_rows(z[None], after(eighths, positions))
    attn_other = swap_cores(attn_own)

    def quarters(first, second, *others):
        asked = jnp.stack([x, y, length, (y + first) & 3, (y + second) & 3, core])
        return attention(
            after(asked.astype(jnp.int32), *others), queries, positions, attn_own, attn_other
        )

    two, one = quarters(2, 1)
    delta_parts = delta_project(scalars, after(pieces, two), delta_own, delta_other)
    three, last = quarters(3, 0, delta_parts)
    delta_mixed = sum_over(delta_parts, "x")
    attn_mixed = sum_over([last, one, two, three], "y")
    return (delta_mixed, attn_mixed, final_state)


def solution(mesh):
    split = Mesh(np.asarray(mesh.devices).reshape(4, 2, 4, 4), ("z", "core", "x", "y"))
    cache, head = ("z", "core"), ("x", "y")
    in_specs = (
        P(cache, None, head),
        P(cache, None, head),
        P(cache, None, head),
        P(cache, None, head),
        P(cache, head, None),
        P(cache, head, None),
        P(cache, head, None, None),
        P(cache, head, None, None),
        P(cache, head, None, None),
        P(cache, None, head),
        P(cache, None, head),
        P(),
        P(),
        P(head, None),
        P(head, None),
    )
    out_specs = (
        P(cache + head, None),
        P(cache + head, None),
        P(cache, head, None, None),
    )
    return jax.shard_map(
        on_device, mesh=split, in_specs=in_specs, out_specs=out_specs, check_vma=False
    )
```

```python
import functools
import math

import jax
import jax.numpy as jnp
import numpy as np
from jax import lax
from jax.experimental import pallas as pl
from jax.experimental.pallas import tpu as pltpu
from jax.sharding import Mesh, PartitionSpec as P

F32 = jnp.float32
BF16 = jnp.bfloat16
CH = 128
HIGH = lax.Precision.HIGHEST
NEG = -1e30
VMEM = 60 * 1024 * 1024


def cost(us):
    return pl.CostEstimate(flops=int(us * 1e9), transcendentals=0, bytes_accessed=int(us * 3e6))


def after(value, *others):
    return lax.optimization_barrier((value, others))[0]


def mm(a, b):
    return lax.dot_general(a, b, (((1,), (0,)), ((), ())), preferred_element_type=F32)


def mm_nt(a, b, precision=None):
    return lax.dot_general(
        a, b, (((1,), (1,)), ((), ())), preferred_element_type=F32, precision=precision
    )


def prep_kernel(q_ref, k_ref, v_ref, b_ref, g_ref, wq_ref, u_ref, p_ref, kt_ref, dec_ref):
    row = lax.broadcasted_iota(jnp.int32, (CH, CH), 0)
    col = lax.broadcasted_iota(jnp.int32, (CH, CH), 1)
    strict = row > col
    incl = row >= col
    diag = row == col
    tri = jnp.where(incl, 1.0, 0.0).astype(F32)
    eye = jnp.where(diag, 1.0, 0.0).astype(F32)
    g8 = jnp.concatenate([g_ref[s] for s in range(4)], axis=0)
    b8 = jnp.concatenate([b_ref[s] for s in range(4)], axis=0)
    g_rows = mm_nt(g8, tri, HIGH)
    g_cols = mm_nt(tri, g8, HIGH)
    b_cols = mm_nt(eye, b8, HIGH)
    chains = []
    for s in range(4):
        k = k_ref[s]
        q = q_ref[s]
        kk = mm_nt(k, k)
        qk = mm_nt(q, k)
        kf = k.astype(F32)
        qf = q.astype(F32)
        rk = lax.rsqrt(jnp.sum(kf * kf, axis=1, keepdims=True) + 1e-6)
        rq = lax.rsqrt(jnp.sum(qf * qf, axis=1, keepdims=True) + 1e-6) * (1.0 / math.sqrt(128.0))
        rk_row = lax.rsqrt(jnp.sum(jnp.where(diag, kk, 0.0), axis=0, keepdims=True) + 1e-6)
        kkn = kk * rk * rk_row
        qkn = qk * rq * rk_row
        kn = kf * rk
        qn = qf * rq
        for h in range(2):
            i = 2 * s + h
            gc = g_cols[:, i : i + 1]
            gr = g_rows[i : i + 1, :]
            bc = b_cols[:, i : i + 1]
            decay = jnp.where(incl, jnp.exp(jnp.where(incl, gc - gr, 0.0)), 0.0)
            low = jnp.where(strict, decay * kkn * bc, 0.0)
            p_ref[0, i] = (decay * qkn).astype(BF16)
            growth = jnp.exp(gc)
            g_last = gr[:, CH - 1 : CH]
            tail = jnp.exp(g_last - gc)
            kt_ref[0, i] = (tail * kn).T.astype(BF16)
            wq_ref[0, i, CH:, :] = (growth * qn).astype(BF16)
            dec_ref[0, i : i + 1, :] = jnp.broadcast_to(jnp.exp(g_last), (1, CH))
            rhs = jnp.concatenate(
                [bc * v_ref[s, :, h * CH : (h + 1) * CH].astype(F32), (bc * growth) * kn], axis=1
            ).astype(BF16)
            chains.append([low, rhs])
    inverses = []
    pair = (row // 2 == col // 2) & strict
    for low, _ in chains:
        inverses.append(eye - jnp.where(pair, low, 0.0))
    m = 2
    while m < CH:
        mask = (row // (2 * m) == col // (2 * m)) & (row // m > col // m)
        lefts = [
            mm(jnp.where(mask, chains[i][0], 0.0).astype(BF16), inverses[i].astype(BF16))
            for i in range(8)
        ]
        steps = [mm(inverses[i].astype(BF16), lefts[i].astype(BF16)) for i in range(8)]
        inverses = [inverses[i] - steps[i] for i in range(8)]
        m *= 2
    for i in range(8):
        solved = mm(inverses[i].astype(BF16), chains[i][1])
        u_ref[0, i] = solved[:, :CH]
        wq_ref[0, i, :CH, :] = solved[:, CH:].astype(BF16)


def prep(delta_query, delta_key, delta_value, strengths, decays):
    chunks = delta_query.shape[1] // CH
    spec_tok = lambda w: pl.BlockSpec((4, CH, w), lambda c: (0, c, 0))
    spec_rate = pl.BlockSpec((4, 2, CH), lambda c: (0, 0, c))
    spec_out = lambda r: pl.BlockSpec((1, 8, r, CH), lambda c: (c, 0, 0, 0))
    shape = lambda r, t: jax.ShapeDtypeStruct((chunks, 8, r, CH), t)
    return pl.pallas_call(
        prep_kernel,
        grid=(chunks,),
        in_specs=[spec_tok(CH), spec_tok(CH), spec_tok(2 * CH), spec_rate, spec_rate],
        out_specs=[
            spec_out(2 * CH),
            spec_out(CH),
            spec_out(CH),
            spec_out(CH),
            pl.BlockSpec((1, 8, CH), lambda c: (c, 0, 0)),
        ],
        out_shape=[
            shape(2 * CH, BF16),
            shape(CH, F32),
            shape(CH, BF16),
            shape(CH, BF16),
            jax.ShapeDtypeStruct((chunks, 8, CH), F32),
        ],
        compiler_params=pltpu.CompilerParams(vmem_limit_bytes=VMEM),
        cost_estimate=cost(0.1),
        name="delta_prep",
    )(delta_query, delta_key, delta_value, strengths, decays)


def scan_kernel(
    src_ref, state_ref, wq_ref, u_ref, p_ref, kt_ref, dec_ref, gate_ref, heads_ref, final_ref, carry
):
    c = pl.program_id(0)

    @pl.when(c == 0)
    def _():
        for s in range(4):
            for h in range(2):
                for j in range(4):
                    block = state_ref[src_ref[s], 32 * h : 32 * h + 32, j * CH : (j + 1) * CH]
                    carry[2 * s + h, 32 * j : 32 * j + 32, :] = block.astype(F32)

    states = [carry[i] for i in range(8)]
    reads = [mm(wq_ref[0, i], states[i].astype(BF16)) for i in range(8)]
    updates = [(u_ref[0, i] - reads[i][:CH]).astype(BF16) for i in range(8)]
    for i in range(8):
        carry[i] = states[i] * dec_ref[0, i : i + 1, :] + mm(kt_ref[0, i], updates[i])
    for i in range(8):
        s, h = i // 2, i % 2
        out = reads[i][CH:] + mm(p_ref[0, i], updates[i])
        scale = lax.rsqrt(jnp.mean(out * out, axis=1, keepdims=True) + 1e-6)
        gate = gate_ref[s, :, h * CH : (h + 1) * CH].astype(F32)
        silu = gate / (1.0 + jnp.exp(-gate))
        heads_ref[0, s, :, h * CH : (h + 1) * CH] = (out * scale * silu).astype(BF16)

    @pl.when(c == pl.num_programs(0) - 1)
    def _():
        for s in range(4):
            for h in range(2):
                final_ref[s, h] = carry[2 * s + h]


def scan(source, arrived, prepared, delta_gate):
    wq, u0, p, kt, dec = prepared
    chunks = wq.shape[0]
    spec = lambda r: pl.BlockSpec((1, 8, r, CH), lambda c, *_: (c, 0, 0, 0))
    return pl.pallas_call(
        scan_kernel,
        grid_spec=pltpu.PrefetchScalarGridSpec(
            num_scalar_prefetch=1,
            grid=(chunks,),
            in_specs=[
                pl.BlockSpec((8, 64, 512), lambda c, *_: (0, 2, 0)),
                spec(2 * CH),
                spec(CH),
                spec(CH),
                spec(CH),
                pl.BlockSpec((1, 8, CH), lambda c, *_: (c, 0, 0)),
                pl.BlockSpec((4, CH, 2 * CH), lambda c, *_: (0, c, 0)),
            ],
            out_specs=[
                pl.BlockSpec((1, 4, CH, 2 * CH), lambda c, *_: (c, 0, 0, 0)),
                pl.BlockSpec((4, 2, CH, CH), lambda c, *_: (0, 0, 0, 0)),
            ],
            scratch_shapes=[pltpu.VMEM((8, CH, CH), F32)],
        ),
        out_shape=[
            jax.ShapeDtypeStruct((chunks, 4, CH, 2 * CH), BF16),
            jax.ShapeDtypeStruct((4, 2, CH, CH), F32),
        ],
        compiler_params=pltpu.CompilerParams(vmem_limit_bytes=VMEM),
        cost_estimate=cost(0.1),
        name="delta_scan",
    )(source, arrived, wq, u0, p, kt, dec, delta_gate)


def swap_halves(core, head):
    low, high = head[:, :CH], head[:, CH:]
    return jnp.concatenate(
        [jnp.where(core == 0, low, high), jnp.where(core == 0, high, low)], axis=1
    )


def delta_project_kernel(sc_ref, h0, h1, h2, h3, own_ref, other_ref, *outs):
    x, core = sc_ref[0], sc_ref[1]
    total = None
    for e, heads_ref in enumerate((h0, h1, h2, h3)):
        rows = jnp.concatenate([heads_ref[(x + d) & 3] for d in range(4)], axis=0)
        weight = jnp.concatenate([own_ref[e], other_ref[e]], axis=0)
        part = mm(swap_halves(core, rows), weight)
        total = part if total is None else total + part
    total = total.astype(BF16)
    for d, ref in enumerate(outs):
        ref[...] = total[d * CH : (d + 1) * CH]


def delta_project(scalars, pieces, own, other):
    weight = pl.BlockSpec((4, CH, 512), lambda i, sc: (0, i, 0))
    return pl.pallas_call(
        delta_project_kernel,
        grid_spec=pltpu.PrefetchScalarGridSpec(
            num_scalar_prefetch=1,
            grid=(4,),
            in_specs=[pl.BlockSpec((4, CH, 2 * CH), lambda i, sc: (0, 0, 0))] * 4 + [weight, weight],
            out_specs=[pl.BlockSpec((CH, 512), lambda i, sc: (0, i))] * 4,
        ),
        out_shape=[jax.ShapeDtypeStruct((CH, 2048), BF16)] * 4,
        compiler_params=pltpu.CompilerParams(vmem_limit_bytes=VMEM),
        cost_estimate=cost(0.1),
        name="delta_project",
    )(scalars, *pieces, own, other)


def pack_kernel(sc_ref, q_ref, g_ref, aw_ref, dw_ref, o0, o1, o2, o3, delta_ref):
    for k, out in enumerate((o0, o1, o2, o3)):
        j = (sc_ref[0] + k) & 3
        out[:512, :256] = q_ref[j]
        out[:512, 256:] = g_ref[j]
        for n in range(4):
            out[512 + n * 32 : 544 + n * 32] = aw_ref[:, n * 512 : (n + 1) * 512]
    for n in range(4):
        delta_ref[n * CH : (n + 1) * CH] = dw_ref[:, n * 512 : (n + 1) * 512]


def pack(scalars, query, gate, attn_weight, delta_weight):
    whole = pl.BlockSpec(query.shape, lambda i, sc: (0, 0, 0))
    return pl.pallas_call(
        pack_kernel,
        grid_spec=pltpu.PrefetchScalarGridSpec(
            num_scalar_prefetch=1,
            grid=(1,),
            in_specs=[
                whole,
                whole,
                pl.BlockSpec((32, 2048), lambda i, sc: (sc[1] * 4 + sc[2], 0)),
                pl.BlockSpec((CH, 2048), lambda i, sc: (sc[1], 0)),
            ],
            out_specs=[pl.BlockSpec((640, 512), lambda i, sc: (0, 0))] * 4
            + [pl.BlockSpec((512, 512), lambda i, sc: (0, 0))],
        ),
        out_shape=[jax.ShapeDtypeStruct((640, 512), BF16)] * 4
        + [jax.ShapeDtypeStruct((512, 512), BF16)],
        compiler_params=pltpu.CompilerParams(vmem_limit_bytes=VMEM),
        cost_estimate=cost(0.1),
        name="pack_queries",
    )(scalars, query, gate, attn_weight, delta_weight)


def stack_kernel(r0, r1, r2, r3, out):
    for k, ref in enumerate((r0, r1, r2, r3)):
        out[k] = ref[...]


def stack_rows(arrays, rows, block):
    return pl.pallas_call(
        stack_kernel,
        grid=(1,),
        in_specs=[pl.BlockSpec((rows, 512), lambda i: (block, 0))] * 4,
        out_specs=pl.BlockSpec((4, rows, 512), lambda i: (0, 0, 0)),
        out_shape=jax.ShapeDtypeStruct((4, rows, 512), BF16),
        compiler_params=pltpu.CompilerParams(vmem_limit_bytes=VMEM),
        cost_estimate=cost(0.1),
        name="stack_weights",
    )(*arrays)


def merge_kernel(sc_ref, r0, r1, r2, r3, out):
    for e, ref in enumerate((r0, r1, r2, r3)):
        at = ((sc_ref[0] - e) & 3) * 32
        for k in range(4):
            for n in range(4):
                rows = pl.ds(pl.multiple_of(n * CH + at, 32), 32)
                out[k, rows] = ref[k, n * 32 : (n + 1) * 32]


def merge_rows(z, arrays):
    vmem = pl.BlockSpec(memory_space=pltpu.VMEM)
    return pl.pallas_call(
        merge_kernel,
        in_specs=[pl.BlockSpec(memory_space=pltpu.SMEM)] + [vmem] * 4,
        out_specs=vmem,
        out_shape=jax.ShapeDtypeStruct((4, 512, 512), BF16),
        compiler_params=pltpu.CompilerParams(vmem_limit_bytes=VMEM),
        cost_estimate=cost(0.1),
        name="merge_weights",
    )(z, *arrays)


def select_kernel(src_ref, landed_ref, fresh_ref, out_ref):
    for j in range(4):
        out_ref[j, :CH] = landed_ref[src_ref[j], :CH]
        out_ref[j, CH:] = fresh_ref[j]


def select(source, landed, fresh):
    vmem = pl.BlockSpec(memory_space=pltpu.VMEM)
    return pl.pallas_call(
        select_kernel,
        in_specs=[pl.BlockSpec(memory_space=pltpu.SMEM), vmem, vmem],
        out_specs=vmem,
        out_shape=jax.ShapeDtypeStruct((4, CH + 64, 512), BF16),
        compiler_params=pltpu.CompilerParams(vmem_limit_bytes=VMEM),
        cost_estimate=cost(0.1),
        name="select_sessions",
    )(source, landed, fresh)


def attention_kernel(
    sc_ref, q0, q1, q2, q3, place_ref, own_hbm, other_hbm, o0, o1, w_ref, w_sem, keys, values, heads
):
    fetches = [
        pltpu.make_async_copy(hbm, w_ref.at[n], w_sem.at[n])
        for n, hbm in enumerate((own_hbm, other_hbm))
    ]
    for fetch in fetches:
        fetch.start()
    length = sc_ref[2]
    rows = 2 * CH
    at_kept = lax.broadcasted_iota(jnp.int32, (1, 256), 1)
    at_fresh = lax.broadcasted_iota(jnp.int32, (1, 128), 1)
    kept_bias, fresh_place = [], []
    for e in range(4):
        ref = place_ref.at[e]
        place = ((at_kept >> 6) * 4 + e) * 64 + (at_kept & 63)
        kept_bias.append(jnp.where(place < length, 0.0, NEG))
        fresh_place.append(((at_fresh >> 5) * 4 + e) * 32 + (at_fresh & 31))
        for j in range(4):
            kept_at, fresh_at = e * 256 + j * 64, 1024 + e * 128 + j * 32
            keys[kept_at : kept_at + 64] = ref[j, :64]
            values[kept_at : kept_at + 64] = ref[j, 64:128]
            keys[fresh_at : fresh_at + 32] = ref[j, 128:160]
            values[fresh_at : fresh_at + 32] = ref[j, 160:]
    kept_bias = jnp.concatenate(kept_bias, axis=1)
    fresh_place = jnp.concatenate(fresh_place, axis=1)
    token = lax.broadcasted_iota(jnp.int32, (rows, 512), 0) & (CH - 1)
    scale = math.log2(math.e) / 16.0

    def load(n, pair, cols):
        at = pl.ds(pl.multiple_of(sc_ref[3 + n] * CH, CH), CH)
        return jnp.concatenate([r[at, cols] for r in pair], axis=0)

    def score(n, pair):
        query = load(n, pair, slice(0, 256))
        return mm_nt(query, keys[:1024]), mm_nt(query, keys[1024:])

    groups = [(n, g) for n in range(2) for g in range(2)]
    pairs = ((q0, q1), (q2, q3))
    ahead = score(0, pairs[0])
    for step, (n, g) in enumerate(groups):
        kept, fresh = ahead
        if step + 1 < len(groups):
            ahead = score(groups[step + 1][0], pairs[groups[step + 1][1]])
        kept = kept + kept_bias
        fresh = jnp.where(fresh_place <= token + sc_ref[3 + n] * CH, fresh, NEG)
        peak = jnp.maximum(
            jnp.max(kept, axis=1, keepdims=True), jnp.max(fresh, axis=1, keepdims=True)
        )
        kept = jnp.exp2((kept - peak) * scale)
        fresh = jnp.exp2((fresh - peak) * scale)
        total = jnp.sum(kept, axis=1, keepdims=True) + jnp.sum(fresh, axis=1, keepdims=True)
        mixed = mm(kept.astype(BF16), values[:1024]) + mm(fresh.astype(BF16), values[1024:])
        gate = load(n, pairs[g], slice(256, 512)).astype(F32)
        gated = (mixed / (total * (1.0 + jnp.exp(-gate)))).astype(BF16)
        for i in range(2):
            k = 2 * g + i
            heads[n * CH : (n + 1) * CH, k * 256 : (k + 1) * 256] = gated[i * CH : (i + 1) * CH]
    for fetch in fetches:
        fetch.wait()
    gated = [swap_halves(sc_ref[5], heads[:, k * 256 : (k + 1) * 256]) for k in range(4)]
    for j in range(4):
        rows = slice(j * CH, (j + 1) * CH)
        out = sum(
            mm(gated[k], jnp.concatenate([w_ref[0, k, rows], w_ref[1, k, rows]], axis=0))
            for k in range(4)
        ).astype(BF16)
        o0[:, j * 512 : (j + 1) * 512] = out[:CH]
        o1[:, j * 512 : (j + 1) * 512] = out[CH:]


def attention(scalars, queries, positions, own, other):
    whole = lambda a: pl.BlockSpec(a.shape, lambda i, sc: (0,) * a.ndim)
    return pl.pallas_call(
        attention_kernel,
        grid_spec=pltpu.PrefetchScalarGridSpec(
            num_scalar_prefetch=1,
            grid=(1,),
            in_specs=[pl.BlockSpec((512, 512), lambda i, sc: (0, 0))] * 4
            + [whole(positions)]
            + [pl.BlockSpec(memory_space=pl.ANY)] * 2,
            out_specs=[pl.BlockSpec((CH, 2048), lambda i, sc: (0, 0))] * 2,
            scratch_shapes=[
                pltpu.VMEM((2, 4, 512, 512), BF16),
                pltpu.SemaphoreType.DMA((2,)),
                pltpu.VMEM((1536, 256), BF16),
                pltpu.VMEM((1536, 256), BF16),
                pltpu.VMEM((2 * CH, 1024), BF16),
            ],
        ),
        out_shape=[jax.ShapeDtypeStruct((CH, 2048), BF16)] * 2,
        compiler_params=pltpu.CompilerParams(vmem_limit_bytes=VMEM),
        cost_estimate=cost(0.1),
        name="attention_project",
    )(scalars, *queries, positions, own, other)


ORDER = (2, 1, 3)


def shift(array, axis, by):
    return lax.ppermute(array, axis, [(i, (i + by) % 4) for i in range(4)])


def row_of(array, index):
    return lax.dynamic_index_in_dim(array, index, 0, keepdims=False)


def all_to_all(array, axis):
    return lax.all_to_all(array, axis, split_axis=0, concat_axis=0, tiled=True)


def sum_over(parts, axis):
    total = parts[0].astype(F32)
    for piece in [shift(parts[d], axis, d) for d in ORDER]:
        total = total + piece.astype(F32)
    return total.astype(BF16)


def regroup(k):
    pairs = []
    for x in range(4):
        for y in range(4):
            a = 2 * (x % 2) + y % 2
            pairs.append((4 * x + y, 4 * ((a + k) % 4) + x // 2 + 2 * (y // 2)))
    return pairs


def on_device(
    delta_query,
    delta_key,
    delta_value,
    delta_gate,
    write_strength,
    decay_log,
    kept_state,
    kept_kv,
    fresh_kv,
    attn_query,
    attn_gate,
    cached_len,
    slot_of_session,
    delta_out_weight,
    attn_out_weight,
):
    count = attn_query.shape[0]
    owners = 8
    owner_id = lax.axis_index(("z", "core"))
    x, y, core = lax.axis_index("x"), lax.axis_index("y"), lax.axis_index("core")
    session_ids = jnp.arange(slot_of_session.shape[0], dtype=jnp.int32)
    on_mine = slot_of_session // count == owner_id
    owner_of = session_ids // count
    wanted = on_mine[None, :] & (owner_of[None, :] == jnp.arange(owners, dtype=jnp.int32)[:, None])
    picked_slot = jnp.sum(jnp.where(wanted, slot_of_session[None, :] - owner_id * count, 0), axis=1)
    source = lax.dynamic_slice_in_dim(slot_of_session, owner_id * count, count) // count
    length = lax.dynamic_index_in_dim(cached_len, owner_id * count + x, 0, keepdims=False)
    source = source.astype(jnp.int32)

    kept_rows = kept_kv.transpose(0, 2, 1, 3).reshape(count, 128, 512)
    state_rows = kept_state.astype(BF16).reshape(count, 2, 4, 32, 128)
    state_rows = state_rows.transpose(0, 1, 3, 2, 4).reshape(count, 64, 512)
    leaving = jnp.take(jnp.concatenate([kept_rows, state_rows], axis=1), picked_slot, axis=0)
    landed = all_to_all(leaving, ("z", "core"))

    z = lax.axis_index("z").astype(jnp.int32)
    place = jnp.stack([2 * (x & 1) + (y & 1), core, z]).astype(jnp.int32)
    *blocks, delta_share = pack(
        after(place, leaving), attn_query, attn_gate, attn_out_weight, delta_out_weight
    )
    def regrouped(array, k):
        return lax.ppermute(array, ("x", "y"), regroup(k))

    def swap_cores(array):
        return lax.ppermute(array, "core", [(0, 1), (1, 0)])

    queries = [regrouped(blocks[k], k) for k in range(4)]

    fresh_rows = fresh_kv.transpose(0, 2, 1, 3).reshape(count, 64, 512)
    landed = after(landed, *blocks)
    chosen = select(source, landed, fresh_rows)
    rows = all_to_all(chosen, "x")
    delta_share = after(delta_share, chosen)
    delta_own = [delta_share] + [shift(delta_share, "y", d) for d in (1, 2, 3)]

    delta_key = after(delta_key, chosen)
    prepared = prep(delta_query, delta_key, delta_value, write_strength, decay_log)
    delta_heads, final_state = scan(source, landed, prepared, delta_gate)
    quarter = [row_of(delta_heads, (y + d) & 3) for d in range(4)]
    pieces = [quarter[0]] + [shift(quarter[d], "y", d) for d in (1, 2, 3)]
    rows = after(rows, delta_heads, *queries)

    low, high = rows[:, :, :256], rows[:, :, 256:]
    leaving = jnp.stack([low, high, low, high], axis=0)
    positions = all_to_all(leaving, "y")

    eighths = stack_rows(after(queries, leaving), CH, 4)
    eighths = [eighths] + [shift(eighths, "z", d) for d in (1, 2, 3)]
    scalars = jnp.stack([x, core]).astype(jnp.int32)
    attn_own = merge_rows(z[None], after(eighths, positions))
    attn_other = swap_cores(attn_own)
    delta_own = stack_rows(after(delta_own, attn_own), 512, 0)
    delta_other = swap_cores(delta_own)

    def quarters(first, second, *others):
        asked = jnp.stack([x, y, length, (y + first) & 3, (y + second) & 3, core])
        return attention(
            after(asked.astype(jnp.int32), *others), queries, positions, attn_own, attn_other
        )

    two, one = quarters(2, 1)
    delta_parts = delta_project(scalars, after(pieces, two), delta_own, delta_other)
    three, last = quarters(3, 0, delta_parts)
    delta_mixed = sum_over(delta_parts, "x")
    attn_mixed = sum_over([last, one, two, three], "y")
    return (delta_mixed, attn_mixed, final_state)


def solution(mesh):
    split = Mesh(np.asarray(mesh.devices).reshape(4, 2, 4, 4), ("z", "core", "x", "y"))
    cache, head = ("z", "core"), ("x", "y")
    in_specs = (
        P(cache, None, head),
        P(cache, None, head),
        P(cache, None, head),
        P(cache, None, head),
        P(cache, head, None),
        P(cache, head, None),
        P(cache, head, None, None),
        P(cache, head, None, None),
        P(cache, head, None, None),
        P(cache, None, head),
        P(cache, None, head),
        P(),
        P(),
        P(head, None),
        P(head, None),
    )
    out_specs = (
        P(cache + head, None),
        P(cache + head, None),
        P(cache, head, None, None),
    )
    return jax.shard_map(
        on_device, mesh=split, in_specs=in_specs, out_specs=out_specs, check_vma=False
    )
```
